256 devices in a mesh: rep: 4 (over z_lo, core), ep: 64 (over y, x, z_hi).
Axes of the slice: x: 4, y: 4, z: 8 (z_hi: 4, z_lo: 2; z = z_hi * 2 + z_lo), core: 2. Of those that a mesh axis runs over, the one named last changes fastest.
Arguments:
- deltas: bfloat16 [4, 64, 2048, 768], P('rep', None, 'ep'), may hold values from -3 to 3
- master: float32 [64, 64, 4, 8, 768], P(None, 'ep', 'rep'), may hold values from -6 to 6
- momentum: float32 [64, 64, 4, 8, 768], P(None, 'ep', 'rep'), may hold values from -3 to 3
- hidden: bfloat16 [4, 8192, 2048], P(None, ('rep', 'ep')), may hold values from -6 to 6
- expert_ids: int32 [4, 8192, 8], P(None, ('rep', 'ep')), may hold values from 0 to 63, as said below
- gate_weights: float32 [4, 8192, 8], P(None, ('rep', 'ep')), may hold values from 0.1 to 0.4
Outputs:
- engine_weights: bfloat16 [64, 2048, 768], P('ep')
- momentum_out: float32 [64, 64, 4, 8, 768], P(None, 'ep', 'rep')
- decoded: bfloat16 [4, 8192, 768], P(None, ('rep', 'ep'))
The draws below stay inside these ranges and needn't reach their ends.
Inputs may be any that keep to these rules, and one draw needn't show every extreme that they name: `expert_ids`: in every step, each row names 8 different experts; among the 32 rows of one device no expert is named by more than 6 rows, and on every device in every step some expert is named by exactly 6 rows.
All inputs are finite; a program needn't handle non-finite values.
Results may differ from the reference program's by a relative error of at most 0.013.
Values may be sent and summed in bfloat16 or wider, within the bound.
No kernel may reach another device: no remote copies, remote signals or barrier semaphores. Data moves between devices by JAX's collectives and lax.ppermute only.
A program may use at most 128 MiB of HBM per device.

```python
import math
import jax
import jax.numpy as jnp
from jax import lax

D = 2048
FF = 768
E = 64
TOP = 8
STEPS = 4
ROWS = 32
CAP = 6
SUB = 8
TOKENS = 8192
N_REP = 4
N_EP = 64


def block_routes(block_key):
    key_units, key_hot, key_count, key_rows, key_cols = jax.random.split(block_key, 5)
    units = E * CAP
    order = jax.random.permutation(key_units, units).astype(jnp.int32)
    unit_rank = jnp.argsort(order).astype(jnp.int32)
    expert_rank = jnp.argsort(jax.random.permutation(key_hot, E).astype(jnp.int32)).astype(jnp.int32)
    hot_count = jax.random.randint(key_count, (), 1, 4).astype(jnp.int32)
    unit_expert = jnp.arange(units, dtype=jnp.int32) // CAP
    is_hot = expert_rank[unit_expert] < hot_count
    score = unit_rank + jnp.where(is_hot, jnp.int32(0), jnp.int32(units))
    chosen = jnp.sort(jnp.argsort(score)[:ROWS * TOP].astype(jnp.int32))
    table = (chosen // CAP).reshape(TOP, ROWS).T
    row_order = jax.random.permutation(key_rows, ROWS).astype(jnp.int32)
    table = table[row_order]
    col_keys = jax.random.split(key_cols, ROWS)
    col_order = jax.vmap(lambda col_key: jax.random.permutation(col_key, TOP).astype(jnp.int32))(col_keys)
    return jnp.take_along_axis(table, col_order, axis=1).astype(jnp.int32)


def draw_expert_ids(key, part):
    key = jax.random.fold_in(key, 7)
    blocks = TOKENS // ROWS

    def one_step(step_index):
        step_key = jax.random.fold_in(key, step_index)
        block_keys = jax.random.split(step_key, blocks)
        routes = jax.vmap(block_routes)(block_keys)
        return routes.reshape(TOKENS, TOP)
    return jax.vmap(one_step)(jnp.arange(STEPS))


def with_spikes(entries, rng, source, target, shards_of, factor):
    owner, partner = [(jnp.arange(entries.shape[axis_at]) // (entries.shape[axis_at] // shards_of)).reshape([-1 if axis == axis_at else 1 for axis in range(entries.ndim)]) for axis_at in (source, target)]
    chosen = jax.random.permutation(rng, shards_of)[partner]
    strong = (owner == chosen) | (owner == (partner + shards_of // 2) % shards_of)
    return jnp.where(strong, factor * entries, entries)


def steps_of(stream_key, dims, cuts, low, largest):
    def one(axis_at, shards_of):
        heights = jax.random.uniform(jax.random.fold_in(jax.random.fold_in(stream_key, 6), axis_at), (shards_of,), jnp.float32, low / len(cuts), largest / len(cuts))
        return jnp.repeat(jnp.exp(heights), dims[axis_at] // shards_of).reshape((-1,) + (1,) * (len(dims) - axis_at - 1))

    gain = one(*cuts[0])
    for cut in cuts[1:]:
        gain = gain * one(*cut)
    return gain


def centred(own_key, extent, width, bound, shards=(), kind=jnp.bfloat16):
    entries = width * jax.random.normal(own_key, extent, jnp.float32)
    if shards:
        entries = entries * steps_of(own_key, extent, shards, -0.22, 0.18)
    return jnp.clip(entries, -bound, bound).astype(kind)


def heavy_noise(key, shape, deviation, most, cuts, heavy, kind=jnp.bfloat16):
    entries = deviation * jax.random.normal(key, shape, jnp.float32)
    if cuts:
        entries = entries * steps_of(key, shape, cuts, -0.22, 0.18)
    return jnp.clip(with_spikes(entries, jax.random.fold_in(key, 3), *heavy), -most, most).astype(kind)


def setup_inputs(seed: int = 0) -> dict:
    keys = jax.random.split(jax.random.key(seed), 7)
    return {
        "deltas": heavy_noise(keys[0], (N_REP, E, D, FF), 0.5, 3.0, ((0, 4), (2, 64)), (0, 2, 4, 2.0)),
        "master": centred(keys[1], (E, N_EP, N_REP, SUB, FF), 1.0, 6.0, ((1, 64), (2, 4)), jnp.float32),
        "momentum": centred(keys[2], (E, N_EP, N_REP, SUB, FF), 0.5, 3.0, ((1, 64), (2, 4)), jnp.float32),
        "hidden": centred(keys[3], (STEPS, TOKENS, D), 1.0, 6.0, ((1, 256),)),
        "expert_ids": draw_expert_ids(jax.random.fold_in(keys[6], 71), 0),
        "gate_weights": jnp.clip(0.1 + 0.3 * jax.random.uniform(keys[5], (STEPS, TOKENS, TOP), jnp.float32) ** steps_of(keys[5], (STEPS, TOKENS, TOP), ((1, 256),), -0.2, 0.2), 0.1, 0.4),
    }


outer_momentum = 0.9
outer_rate = 0.7

def outer_step(deltas, master, momentum):
    params = master.reshape(E, D, FF)
    velocity_old = momentum.reshape(E, D, FF)
    summed = deltas[0].astype(jnp.float32)
    for replica in range(1, N_REP):
        summed = summed + deltas[replica].astype(jnp.float32)
    outer_grad = summed / N_REP
    velocity = outer_momentum * velocity_old + outer_grad
    engine = (params - outer_rate * (outer_grad + outer_momentum * velocity)).astype(jnp.bfloat16)
    return (engine, velocity.reshape(momentum.shape))

def decode_step(engine, inputs_now, route_ids, route_gates):
    row_limit = TOKENS // ROWS * CAP
    inv_root = 1.0 / math.sqrt(D)

    def one_expert(expert):
        matches = route_ids == expert
        row_hit = jnp.any(matches, axis=1)
        picked = jnp.nonzero(row_hit, size=row_limit, fill_value=0)[0]
        hit_count = jnp.sum(row_hit.astype(jnp.int32))
        in_range = (jnp.arange(row_limit) < hit_count).astype(jnp.float32)
        weight = lax.optimization_barrier(jnp.sum(jnp.where(matches, route_gates, jnp.float32(0.0)), axis=1))[picked] * in_range
        product = jnp.dot(inputs_now[picked], engine[expert], preferred_element_type=jnp.float32) * inv_root
        expert_hidden = jax.nn.silu(product).astype(jnp.bfloat16)
        return (picked, weight[:, None] * expert_hidden.astype(jnp.float32))
    picked, weighted = lax.map(one_expert, jnp.arange(E))
    summed = jnp.zeros((TOKENS, FF), jnp.float32).at[picked.reshape(-1)].add(weighted.reshape(-1, FF))
    return summed.astype(jnp.bfloat16)

def reference(deltas, master, momentum, hidden, expert_ids, gate_weights):
    engine, velocity = outer_step(deltas, master, momentum)
    decoded = jnp.stack([decode_step(engine, hidden[step_index], expert_ids[step_index], gate_weights[step_index]) for step_index in range(STEPS)])
    return (engine, velocity, decoded)
```

```python
import math

import jax
import jax.numpy as jnp
from jax import lax
from jax.sharding import Mesh, PartitionSpec as P

outer_momentum = 0.9
outer_rate = 0.7

RING = 4
PLUS = [(i, (i + 1) % RING) for i in range(RING)]
MINUS = [(i, (i - 1) % RING) for i in range(RING)]
SWAP = [(0, 1), (1, 0)]


def swap(value, axis):
    return lax.ppermute(value, axis, SWAP)


def ring_gather(value, axis):
    half = value.shape[0] // 2
    before = lax.ppermute(value, axis, PLUS)
    after = lax.ppermute(value, axis, MINUS)
    far_low = lax.ppermute(before[:half], axis, PLUS)
    far_high = lax.ppermute(after[half:], axis, MINUS)
    return value, before, after, (far_low, far_high)


def ring_scatter(own, before, after, far, axis):
    half = far.shape[0] // 2
    low = lax.ppermute(far[:half].astype(jnp.bfloat16), axis, PLUS)
    high = lax.ppermute(far[half:].astype(jnp.bfloat16), axis, MINUS)
    after = jnp.concatenate([after[:half] + low.astype(jnp.float32), after[half:]])
    before = jnp.concatenate([before[:half], before[half:] + high.astype(jnp.float32)])
    from_before = lax.ppermute(after.astype(jnp.bfloat16), axis, PLUS)
    from_after = lax.ppermute(before.astype(jnp.bfloat16), axis, MINUS)
    return own + from_before.astype(jnp.float32) + from_after.astype(jnp.float32)


def in_order(position, mine, other, axis):
    return jnp.where(
        position == 0,
        jnp.stack([mine, other], axis=axis),
        jnp.stack([other, mine], axis=axis),
    )


def at_offsets(value, position, axis):
    order = (position + jnp.array([0, 3, 1, 2], jnp.int32)) % RING
    return jnp.take(value, order, axis=axis)


def local(deltas, master, momentum, hidden, expert_ids, gate_weights):
    experts, block_rows, width = deltas.shape[1:]
    sub = master.shape[3]
    steps, rows, model = hidden.shape
    top = expert_ids.shape[2]
    z_lo, core = lax.axis_index("z_lo"), lax.axis_index("core")
    y, x, z_hi = lax.axis_index("y"), lax.axis_index("x"), lax.axis_index("z_hi")
    half_width = width // 2
    taken = steps * rows

    pieces = deltas[0].reshape(experts, 2, 2, sub, width)
    kept = lax.dynamic_index_in_dim(pieces, core, axis=2, keepdims=False)
    given = lax.dynamic_index_in_dim(pieces, 1 - core, axis=2, keepdims=False)
    pair = kept.astype(jnp.float32) + swap(given, "core").astype(jnp.float32)
    kept = lax.dynamic_index_in_dim(pair, z_lo, axis=1, keepdims=False)
    given = lax.dynamic_index_in_dim(pair, 1 - z_lo, axis=1, keepdims=False)
    summed = kept + swap(given.astype(jnp.bfloat16), "z_lo").astype(jnp.float32)
    params = master.reshape(experts, sub, width)
    velocity_old = momentum.reshape(experts, sub, width)
    outer_grad = summed / 4
    velocity = outer_momentum * velocity_old + outer_grad
    piece = (params - outer_rate * (outer_grad + outer_momentum * velocity)).astype(jnp.bfloat16)

    mine = lax.all_to_all(piece, ("y", "x", "z_hi"), split_axis=0, concat_axis=0, tiled=True)
    mine = in_order(z_lo, mine, swap(mine, "z_lo"), 1)
    mine = in_order(core, mine, swap(mine, "core"), 2)
    engine = mine.reshape(model, width)

    part = lax.dynamic_slice_in_dim(engine, core * half_width, half_width, axis=1)
    own, before, after, far = ring_gather(part, "x")
    weights = [own, before, after, jnp.concatenate(far)]
    offsets = [0, 3, 1, 2]

    flat = hidden.reshape(taken, model)
    own, before, after, far = ring_gather(flat, "z_hi")
    plane = jnp.concatenate([own, before, after, *far])
    own, before, after, far = ring_gather(plane, "y")
    plane = jnp.concatenate([own, before, after, *far])
    plane = jnp.concatenate([plane, swap(plane, "core")])

    routes = jnp.concatenate([expert_ids.astype(jnp.float32), gate_weights], axis=-1)
    routes = routes.reshape(taken, 2 * top)
    routes = lax.all_gather(routes, ("core", "y", "z_hi"), axis=0).reshape(2, RING, RING, taken, 2 * top)
    routes = jnp.take(routes, (core + jnp.arange(2, dtype=jnp.int32)) % 2, axis=0)
    routes = at_offsets(at_offsets(routes, y, 1), z_hi, 2).reshape(-1, 2 * top)
    ids, gates = routes[:, :top].astype(jnp.int32), routes[:, top:]

    total = None
    inv_root = 1.0 / math.sqrt(model)
    for offset, weight in zip(offsets, weights):
        expert = (y * RING + (x + offset) % RING) * RING + z_hi
        gate = jnp.sum(jnp.where(ids == expert, gates, 0.0), axis=1)
        product = jnp.dot(plane, weight, preferred_element_type=jnp.float32)
        answer = jax.nn.silu(product * inv_root).astype(jnp.bfloat16).astype(jnp.float32)
        term = gate[:, None] * answer
        total = term if total is None else total + term

    total = total.reshape(2, RING, RING, taken, half_width).transpose(1, 2, 0, 3, 4)
    total = total.reshape(RING, RING, 2 * taken, half_width)
    ringed = ring_scatter(
        *[total[i].reshape(RING * 2 * taken, half_width) for i in range(RING)], "y"
    ).reshape(RING, 2 * taken, half_width)
    ringed = ring_scatter(*[ringed[i] for i in range(RING)], "z_hi").reshape(2, taken, half_width)
    mine, other = ringed[0], swap(ringed[1].astype(jnp.bfloat16), "core").astype(jnp.float32)
    decoded = in_order(core, mine, other, 1).reshape(steps, rows, width).astype(jnp.bfloat16)
    return (engine[None], velocity.reshape(momentum.shape), decoded)


def solution(mesh):
    fine = Mesh(
        mesh.devices.reshape(2, 2, RING, RING, RING), ("z_lo", "core", "y", "x", "z_hi")
    )
    rep, ep = ("z_lo", "core"), ("y", "x", "z_hi")
    return jax.shard_map(
        local,
        mesh=fine,
        in_specs=(
            P(rep, None, ep, None),
            P(None, ep, rep, None, None),
            P(None, ep, rep, None, None),
            P(None, rep + ep, None),
            P(None, rep + ep, None),
            P(None, rep + ep, None),
        ),
        out_specs=(
            P(ep, None, None),
            P(None, ep, rep, None, None),
            P(None, rep + ep, None),
        ),
        check_vma=False,
    )
```

```python
import math

import jax
import jax.numpy as jnp
from jax import lax
from jax.sharding import Mesh, PartitionSpec as P

outer_momentum = 0.9
outer_rate = 0.7

RING = 4
PLUS = [(i, (i + 1) % RING) for i in range(RING)]
MINUS = [(i, (i - 1) % RING) for i in range(RING)]
SWAP = [(0, 1), (1, 0)]


def swap(value, axis):
    return lax.ppermute(value, axis, SWAP)


def tie(*values):
    return lax.optimization_barrier(values)


def forward(before, after, axis):
    half = before.shape[0] // 2
    low = lax.ppermute(before[:half], axis, PLUS)
    high = lax.ppermute(after[half:], axis, MINUS)
    return jnp.concatenate([low, high])


def neighbours(value, axis):
    return lax.ppermute(value, axis, PLUS), lax.ppermute(value, axis, MINUS)


def ring_scatter(own, before, after, far, axis):
    half = far.shape[0] // 2
    low = lax.ppermute(far[:half].astype(jnp.bfloat16), axis, PLUS)
    high = lax.ppermute(far[half:].astype(jnp.bfloat16), axis, MINUS)
    after = jnp.concatenate([after[:half] + low.astype(jnp.float32), after[half:]])
    before = jnp.concatenate([before[:half], before[half:] + high.astype(jnp.float32)])
    from_before = lax.ppermute(after.astype(jnp.bfloat16), axis, PLUS)
    from_after = lax.ppermute(before.astype(jnp.bfloat16), axis, MINUS)
    return own + from_before.astype(jnp.float32) + from_after.astype(jnp.float32)


def in_order(position, mine, other, axis):
    return jnp.where(
        position == 0,
        jnp.stack([mine, other], axis=axis),
        jnp.stack([other, mine], axis=axis),
    )


def local(deltas, master, momentum, hidden, expert_ids, gate_weights):
    experts, block_rows, width = deltas.shape[1:]
    sub = master.shape[3]
    steps, rows, model = hidden.shape
    top = expert_ids.shape[2]
    z_lo, core = lax.axis_index("z_lo"), lax.axis_index("core")
    y, x, z_hi = lax.axis_index("y"), lax.axis_index("x"), lax.axis_index("z_hi")
    taken = steps * rows

    flat = hidden.reshape(taken, model)
    routes = jnp.concatenate([expert_ids.astype(jnp.float32), gate_weights], axis=-1)
    routes = routes.reshape(taken, 2 * top)
    before, after = neighbours(flat, "z_hi")
    routes_before, routes_after = neighbours(routes, "z_hi")

    pieces = deltas[0].reshape(experts, 2, 2, sub, width)
    kept = lax.dynamic_index_in_dim(pieces, core, axis=2, keepdims=False)
    given = lax.dynamic_index_in_dim(pieces, 1 - core, axis=2, keepdims=False)
    pair = kept.astype(jnp.float32) + swap(given, "core").astype(jnp.float32)
    kept = lax.dynamic_index_in_dim(pair, z_lo, axis=1, keepdims=False)
    given = lax.dynamic_index_in_dim(pair, 1 - z_lo, axis=1, keepdims=False)
    given = given.astype(jnp.bfloat16)
    given, before, after, routes_before, routes_after = tie(
        given, before, after, routes_before, routes_after
    )
    received = swap(given, "z_lo")
    far = forward(before, after, "z_hi")
    routes_far = forward(routes_before, routes_after, "z_hi")
    plane = jnp.concatenate([flat, before, after, far])
    routes = jnp.concatenate([routes, routes_before, routes_after, routes_far])
    received, plane, routes = tie(received, plane, routes)

    summed = kept + received.astype(jnp.float32)
    params = master.reshape(experts, sub, width)
    velocity_old = momentum.reshape(experts, sub, width)
    outer_grad = summed / 4
    velocity = outer_momentum * velocity_old + outer_grad
    piece = (params - outer_rate * (outer_grad + outer_momentum * velocity)).astype(jnp.bfloat16)

    before, after = neighbours(plane, "y")
    routes_before, routes_after = neighbours(routes, "y")

    first = lax.all_to_all(piece, ("y", "x", "z_hi"), split_axis=0, concat_axis=0, tiled=True)
    second = swap(first, "z_lo")
    first_before, first_after = neighbours(first, "x")
    first_before, first_after, second, before, after, routes_before, routes_after = tie(
        first_before, first_after, second, before, after, routes_before, routes_after
    )
    first_far = forward(first_before, first_after, "x")
    second_before, second_after = neighbours(second, "x")
    far = forward(before, after, "y")
    routes_far = forward(routes_before, routes_after, "y")
    second_far = forward(second_before, second_after, "x")

    def whole(one, two):
        part = in_order(z_lo, one, two, 1)
        return in_order(core, part, swap(part, "core"), 2).reshape(model, width)

    engine = whole(first, second)
    weights = [
        engine,
        whole(first_before, second_before),
        whole(first_after, second_after),
        whole(first_far, second_far),
    ]
    blocks = [plane, before, after, far]
    routes = [routes, routes_before, routes_after, routes_far]

    inv_root = 1.0 / math.sqrt(model)
    totals = []
    for block, route in zip(blocks, routes):
        ids, gates = route[:, :top].astype(jnp.int32), route[:, top:]
        total = None
        for offset, weight in zip([0, 3, 1, 2], weights):
            expert = (y * RING + (x + offset) % RING) * RING + z_hi
            gate = jnp.sum(jnp.where(ids == expert, gates, 0.0), axis=1)
            product = jnp.dot(block, weight, preferred_element_type=jnp.float32)
            answer = jax.nn.silu(product * inv_root).astype(jnp.bfloat16).astype(jnp.float32)
            term = gate[:, None] * answer
            total = term if total is None else total + term
        totals.append(total)

    ringed = ring_scatter(*totals, "y").reshape(RING, taken, width)
    decoded = ring_scatter(*[ringed[i] for i in range(RING)], "z_hi")
    decoded = decoded.reshape(steps, rows, width).astype(jnp.bfloat16)
    return (engine[None], velocity.reshape(momentum.shape), decoded)


def solution(mesh):
    fine = Mesh(
        mesh.devices.reshape(2, 2, RING, RING, RING), ("z_lo", "core", "y", "x", "z_hi")
    )
    rep, ep = ("z_lo", "core"), ("y", "x", "z_hi")
    return jax.shard_map(
        local,
        mesh=fine,
        in_specs=(
            P(rep, None, ep, None),
            P(None, ep, rep, None, None),
            P(None, ep, rep, None, None),
            P(None, rep + ep, None),
            P(None, rep + ep, None),
            P(None, rep + ep, None),
        ),
        out_specs=(
            P(ep, None, None),
            P(None, ep, rep, None, None),
            P(None, rep + ep, None),
        ),
        check_vma=False,
    )
```

```python
import functools
import math

import jax
import jax.numpy as jnp
from jax import lax
from jax.experimental import pallas as pl
from jax.experimental.layout import Layout, with_layout_constraint
from jax.experimental.pallas import tpu as pltpu
from jax.sharding import Mesh, PartitionSpec as P

outer_momentum = 0.9
outer_rate = 0.7

RING = 4
LANES = 128
GROUP = 256
PLUS = [(i, (i + 1) % RING) for i in range(RING)]
MINUS = [(i, (i - 1) % RING) for i in range(RING)]
CHIPS = 8
Z = ("z_lo", "z_hi")
UP = [(i % 2 * RING + i // 2, (i + 1) % CHIPS % 2 * RING + (i + 1) % CHIPS // 2) for i in range(CHIPS)]
DOWN = [(after, before) for before, after in UP]
SWAP = [(0, 1), (1, 0)]


def swap(value, axis):
    return lax.ppermute(value, axis, SWAP)


def later(value, *first):
    return lax.optimization_barrier((value,) + first)[0]


def neighbours(value, axis):
    return lax.ppermute(value, axis, PLUS), lax.ppermute(value, axis, MINUS)


def forward(before, after, axis):
    half = before.shape[0] // 2
    low = lax.ppermute(before[:half], axis, PLUS)
    high = lax.ppermute(after[half:], axis, MINUS)
    return jnp.concatenate([low, high])


def far_sums(before, after, far, axis):
    half = far.shape[0] // 2
    low = lax.ppermute(far[:half].astype(jnp.bfloat16), axis, PLUS)
    high = lax.ppermute(far[half:].astype(jnp.bfloat16), axis, MINUS)
    after = jnp.concatenate([after[:half] + low.astype(jnp.float32), after[half:]])
    before = jnp.concatenate([before[:half], before[half:] + high.astype(jnp.float32)])
    return before.astype(jnp.bfloat16), after.astype(jnp.bfloat16)


def near_sums(own, before, after, axis):
    from_before = lax.ppermute(after, axis, PLUS)
    from_after = lax.ppermute(before, axis, MINUS)
    return own + from_before.astype(jnp.float32) + from_after.astype(jnp.float32)


def by_core(core, mine, other, axis):
    return jnp.where(
        core == 0,
        jnp.concatenate([mine, other], axis=axis),
        jnp.concatenate([other, mine], axis=axis),
    )


def rounded(value):
    return lax.reduce_precision(value, exponent_bits=8, mantissa_bits=7)


def expert_kernel(top, scale, where_ref, own_ref, other_ref, weight_ref, out_ref):
    model, wide = weight_ref.shape[0], weight_ref.shape[1] // RING
    here = where_ref[1]

    def rows(ref):
        routing = ref[:, model : model + LANES].astype(jnp.float32)
        ids = routing[:, :top]
        gates = routing[:, top : 2 * top] + routing[:, 2 * top : 3 * top]
        gates = gates + routing[:, 3 * top : 4 * top]
        rows_in = ref[:, :model]
        total = None
        for group in range(0, RING * wide, GROUP):
            product = jnp.dot(
                rows_in, weight_ref[:, group : group + GROUP], preferred_element_type=jnp.float32
            )
            for start in range(0, GROUP, wide):
                offset = (group + start) // wide
                named = ids == (here + offset).astype(jnp.float32)
                gate = jnp.sum(jnp.where(named, gates, 0.0), axis=1, keepdims=True)
                value = product[:, start : start + wide] * (0.5 * scale)
                answer = value + value * jnp.tanh(value)
                answer = gate * answer.astype(jnp.bfloat16).astype(jnp.float32)
                total = answer if total is None else total + answer
        out_ref[...] = total.astype(out_ref.dtype)

    @pl.when(pl.program_id(0) == 0)
    def _():
        rows(own_ref)

    @pl.when(pl.program_id(0) == 1)
    def _():
        rows(other_ref)


def expert_terms(where, own, other, weight, top, dtype):
    count, columns = own.shape[0] // RING, own.shape[1]
    model, wide = weight.shape[0], weight.shape[1] // RING
    tile = math.gcd(count, 256)
    tiles = count // tile
    return pl.pallas_call(
        functools.partial(expert_kernel, top, 1.0 / math.sqrt(model)),
        grid_spec=pltpu.PrefetchScalarGridSpec(
            num_scalar_prefetch=1,
            grid=(2, tiles),
            in_specs=[
                pl.BlockSpec(
                    (tile, columns),
                    lambda side, i, where: (where[0] * tiles + jnp.where(side == 0, i, tiles - 1), 0),
                ),
                pl.BlockSpec(
                    (tile, columns),
                    lambda side, i, where: (where[0] * tiles + jnp.where(side == 0, 0, i), 0),
                ),
                pl.BlockSpec((model, RING * wide), lambda side, i, where: (0, 0)),
            ],
            out_specs=pl.BlockSpec((tile, wide), lambda side, i, where: (side * tiles + i, 0)),
        ),
        out_shape=jax.ShapeDtypeStruct((2 * count, wide), dtype),
        compiler_params=pltpu.CompilerParams(vmem_limit_bytes=18 * 2**20),
        cost_estimate=pl.CostEstimate(
            flops=4 * count * model * RING * wide,
            bytes_accessed=2 * (2 * count * columns + model * RING * wide),
            transcendentals=2 * count * RING * wide,
        ),
    )(where, own, other, weight)


def local(deltas, master, momentum, hidden, expert_ids, gate_weights):
    experts, block_rows, width = deltas.shape[1:]
    sub = master.shape[3]
    steps, rows, model = hidden.shape
    top = expert_ids.shape[2]
    z_lo, core = lax.axis_index("z_lo"), lax.axis_index("core")
    y, x, z_hi = lax.axis_index("y"), lax.axis_index("x"), lax.axis_index("z_hi")
    z = z_hi * 2 + z_lo
    taken = steps * rows
    owners = RING * RING
    span = owners * sub
    half_width = width // 2
    cut = 2 * half_width // 3
    parts = [(0, cut), (cut, half_width)]

    pieces = deltas[0].reshape(experts, 2, 2, sub, width)
    kept = lax.dynamic_index_in_dim(pieces, core, axis=2, keepdims=False)
    given = lax.dynamic_index_in_dim(pieces, 1 - core, axis=2, keepdims=False)
    pair = kept.astype(jnp.float32) + swap(given, "core").astype(jnp.float32)
    kept = lax.dynamic_index_in_dim(pair, z_lo, axis=1, keepdims=False)
    given = lax.dynamic_index_in_dim(pair, 1 - z_lo, axis=1, keepdims=False).astype(jnp.bfloat16)
    received = swap(given, "z_lo")
    hidden, expert_ids, gate_weights = [
        later(value, given) for value in (hidden, expert_ids, gate_weights)
    ]

    gate_high = rounded(gate_weights)
    gate_mid = rounded(gate_weights - gate_high)
    gate_low = gate_weights - gate_high - gate_mid
    routing = jnp.concatenate(
        [expert_ids.astype(jnp.float32), gate_high, gate_mid, gate_low], axis=-1
    ).astype(jnp.bfloat16)
    routing = jnp.pad(routing.reshape(taken, 4 * top), ((0, 0), (0, LANES - 4 * top)))
    place = jnp.arange(model, dtype=jnp.int32)
    ring_z = (z - 3 + place // (2 * span)) % CHIPS
    source = (place // sub % owners) * RING + ring_z // 2
    source = source * block_rows + (ring_z % 2) * 2 * sub + (place // span % 2) * sub + place % sub
    ordering = (jnp.arange(model, dtype=jnp.int32)[:, None] == source[None, :]).astype(jnp.bfloat16)
    flat = jnp.dot(
        hidden.reshape(taken, model), ordering, preferred_element_type=jnp.float32
    ).astype(jnp.bfloat16)
    flat = jnp.concatenate([flat, routing], axis=1)
    flat = with_layout_constraint(flat, Layout(major_to_minor=(0, 1)))

    plane = lax.all_gather(flat, ("y", "x"), axis=0, tiled=True)
    params = master.reshape(experts, sub, width)
    velocity_old = momentum.reshape(experts, sub, width)
    outer_grad = (kept + received.astype(jnp.float32)) / 4
    velocity = outer_momentum * velocity_old + outer_grad
    piece = (params - outer_rate * (outer_grad + outer_momentum * velocity)).astype(jnp.bfloat16)

    piece = piece.reshape(owners, RING, sub, 2, half_width)
    piece = jnp.concatenate(
        [
            piece[..., start:stop].transpose(0, 2, 3, 1, 4).reshape(owners, sub, 2, -1)
            for start, stop in parts
        ],
        axis=-1,
    ).reshape(owners, sub, 2 * RING * half_width)
    piece = lax.all_to_all(piece, ("y", "x"), split_axis=0, concat_axis=0, tiled=True)
    piece = piece.reshape(span, 2 * RING * half_width)
    mine = lax.dynamic_slice_in_dim(piece, core * RING * half_width, RING * half_width, axis=1)
    other = lax.dynamic_slice_in_dim(piece, (1 - core) * RING * half_width, RING * half_width, axis=1)
    piece = by_core(core, mine, swap(other, "core"), 0)
    piece_a, piece_b = piece[:, : RING * cut], piece[:, RING * cut :]

    def hop(up, down):
        return lax.ppermute(up, Z, UP), lax.ppermute(down, Z, DOWN)

    def z_ring(piece, waits=((), (), (), ())):
        steps_made = []
        up, down = piece, piece
        for first in waits[:3]:
            up, down = hop(later(up, *first), later(down, *first))
            steps_made.append((up, down))
        low, high = hop(later(up[:span], *waits[3]), later(down[span:], *waits[3]))
        (up1, down1), (up2, down2), (up3, down3) = steps_made
        return [up3, up2, up1, piece, down1, down2, down3, low, high]

    ring_a = z_ring(piece_a)
    ring_b = z_ring(piece_b, ((ring_a[2], ring_a[4]), (), (), ()))
    plane = later(plane, ring_a[1], ring_a[5])
    beside = swap(plane, "core")

    def terms(weight):
        return [
            expert_terms(
                jnp.stack([(y + offset) % RING, (y * RING + x) * RING]),
                plane, beside, weight, top, jnp.bfloat16 if offset == 2 else jnp.float32,
            )
            for offset in (0, 3, 1, 2)
        ]

    def to_rows(ringed):
        wide = ringed.shape[1]
        ringed = ringed.reshape(2, RING, taken, wide)
        own, before, after, far = [
            lax.dynamic_index_in_dim(ringed, (x + offset) % RING, axis=1, keepdims=False)
            for offset in (0, 3, 1, 2)
        ]
        received = [
            lax.ppermute(far.astype(jnp.bfloat16), "x", [(i, (i + 2) % RING) for i in range(RING)]),
            lax.ppermute(after.astype(jnp.bfloat16), "x", PLUS),
            lax.ppermute(before.astype(jnp.bfloat16), "x", MINUS),
        ]
        for value in received:
            own = own + value.astype(jnp.float32)
        return own[0], swap(own[1].astype(jnp.bfloat16), "core").astype(jnp.float32)

    weight_a = jnp.concatenate(ring_a)
    own, before, after, far = terms(weight_a)
    weight_b = jnp.concatenate(ring_b)
    before, after = far_sums(before, after, far, "y")
    weight_b = later(weight_b, before, after, own)
    mine_a, other_a = to_rows(near_sums(own, before, after, "y"))
    own, before, after, far = terms(weight_b)
    before, after = far_sums(before, after, far, "y")

    def served(weight):
        wide = weight.shape[1] // RING
        return lax.dynamic_slice_in_dim(weight, z_hi * wide, wide, axis=1)

    mine = jnp.concatenate([served(weight_a), served(weight_b)], axis=1)
    mine = later(mine, own)
    engine = by_core(core, mine, swap(mine, "core"), 1)
    engine = engine.reshape(CHIPS, 2, owners, sub, width)
    engine = jnp.concatenate([engine, engine])
    engine = lax.dynamic_slice_in_dim(engine, (CHIPS + 3 - z) % CHIPS, CHIPS, axis=0)
    engine = engine.transpose(2, 0, 1, 3, 4).reshape(model, width)

    mine_b, other_b = to_rows(near_sums(own, before, after, "y"))
    mine = jnp.concatenate([mine_a, mine_b], axis=1)
    other = jnp.concatenate([other_a, other_b], axis=1)
    decoded = by_core(core, mine, other, 1).reshape(steps, rows, width).astype(jnp.bfloat16)
    return (engine[None], velocity.reshape(momentum.shape), decoded)


def solution(mesh):
    fine = Mesh(
        mesh.devices.reshape(2, 2, RING, RING, RING), ("z_lo", "core", "y", "x", "z_hi")
    )
    rep, ep = ("z_lo", "core"), ("y", "x", "z_hi")
    return jax.shard_map(
        local,
        mesh=fine,
        in_specs=(
            P(rep, None, ep, None),
            P(None, ep, rep, None, None),
            P(None, ep, rep, None, None),
            P(None, rep + ep, None),
            P(None, rep + ep, None),
            P(None, rep + ep, None),
        ),
        out_specs=(
            P(ep, None, None),
            P(None, ep, rep, None, None),
            P(None, rep + ep, None),
        ),
        check_vma=False,
    )
```

```python
import functools
import math

import jax
import jax.numpy as jnp
from jax import lax
from jax.experimental import pallas as pl
from jax.experimental.layout import Layout, with_layout_constraint
from jax.experimental.pallas import tpu as pltpu
from jax.sharding import Mesh, PartitionSpec as P

outer_momentum = 0.9
outer_rate = 0.7

RING = 4
LANES = 128
CAP = 6
GROUPS = 8
PLUS = [(i, (i + 1) % RING) for i in range(RING)]
MINUS = [(i, (i - 1) % RING) for i in range(RING)]
CHIPS = 8
Z = ("z_lo", "z_hi")
UP = [(i % 2 * RING + i // 2, (i + 1) % CHIPS % 2 * RING + (i + 1) % CHIPS // 2) for i in range(CHIPS)]
DOWN = [(after, before) for before, after in UP]
SWAP = [(0, 1), (1, 0)]


def swap(value, axis):
    return lax.ppermute(value, axis, SWAP)


def later(value, *first):
    return lax.optimization_barrier((value,) + first)[0]


def neighbours(value, axis):
    return lax.ppermute(value, axis, PLUS), lax.ppermute(value, axis, MINUS)


def forward(before, after, axis):
    half = before.shape[0] // 2
    low = lax.ppermute(before[:half], axis, PLUS)
    high = lax.ppermute(after[half:], axis, MINUS)
    return jnp.concatenate([low, high])


def far_sums(before, after, far, axis):
    half = far.shape[0] // 2
    low = lax.ppermute(far[:half].astype(jnp.bfloat16), axis, PLUS)
    high = lax.ppermute(far[half:].astype(jnp.bfloat16), axis, MINUS)
    after = jnp.concatenate([after[:half] + low.astype(jnp.float32), after[half:]])
    before = jnp.concatenate([before[:half], before[half:] + high.astype(jnp.float32)])
    return before.astype(jnp.bfloat16), after.astype(jnp.bfloat16)


def near_sums(own, before, after, axis):
    from_before = lax.ppermute(after, axis, PLUS)
    from_after = lax.ppermute(before, axis, MINUS)
    return own + from_before.astype(jnp.float32) + from_after.astype(jnp.float32)


def by_core(core, mine, other, axis):
    return jnp.where(
        core == 0,
        jnp.concatenate([mine, other], axis=axis),
        jnp.concatenate([other, mine], axis=axis),
    )


def rounded(value):
    return lax.reduce_precision(value, exponent_bits=8, mantissa_bits=7)


def pack_kernel(top, where_ref, row_ref, low_ref, high_ref, spread_ref):
    count, model, slots = row_ref.shape[0], low_ref.shape[2], low_ref.shape[1]
    wide = RING * slots
    routing = row_ref[:, model : model + LANES].astype(jnp.float32)
    place = jnp.where(routing[:, :top] == where_ref[0].astype(jnp.float32), routing[:, top : 2 * top], -wide - 1.0)
    lane = lax.broadcasted_iota(jnp.int32, (count, 2 * wide), 1).astype(jnp.float32)
    spread = jnp.zeros((count, 2 * wide), jnp.float32)
    placed = jnp.zeros((count, wide), jnp.float32)
    for choice in range(top):
        here = place[:, choice : choice + 1]
        high = routing[:, 2 * top + choice : 2 * top + choice + 1]
        rest = routing[:, 3 * top + choice : 3 * top + choice + 1]
        spread = jnp.where(lane == here, high, jnp.where(lane == here + wide, rest, spread))
        placed = jnp.where(lane[:, :wide] == here, 1.0, placed)
    spread_ref[...] = spread.astype(jnp.bfloat16)
    packed = lax.dot_general(
        placed.astype(jnp.bfloat16),
        row_ref[:, :model],
        (((0,), (0,)), ((), ())),
        preferred_element_type=jnp.float32,
    ).astype(jnp.bfloat16)
    for offset in range(RING):
        (low_ref, high_ref)[offset // 2][offset % 2] = packed[offset * slots : (offset + 1) * slots]


def pack(where, plane, model, top, rows):
    count, columns = plane.shape
    tile = GROUPS * rows
    tiles = count // tile
    slots = GROUPS * CAP
    return pl.pallas_call(
        functools.partial(pack_kernel, top),
        grid=(tiles,),
        in_specs=[
            pl.BlockSpec(memory_space=pltpu.SMEM),
            pl.BlockSpec((tile, columns), lambda i: (i, 0)),
        ],
        out_specs=[pl.BlockSpec((2, slots, model), lambda i: (0, i, 0))] * 2
        + [pl.BlockSpec((tile, 2 * RING * slots), lambda i: (i, 0))],
        out_shape=[jax.ShapeDtypeStruct((2, tiles * slots, model), jnp.bfloat16)] * 2
        + [jax.ShapeDtypeStruct((count, 2 * RING * slots), jnp.bfloat16)],
        compiler_params=pltpu.CompilerParams(vmem_limit_bytes=18 * 2**20),
        cost_estimate=pl.CostEstimate(
            flops=2 * count * RING * slots * model,
            bytes_accessed=2 * count * columns + 2 * tiles * slots * RING * model,
            transcendentals=0,
        ),
    )(where, plane)


def answers_kernel(scale, own_ref, other_ref, weight_ref, out_ref):
    count = own_ref.shape[1]
    for side, ref in enumerate((own_ref, other_ref)):
        product = jnp.dot(ref[0], weight_ref[...], preferred_element_type=jnp.float32)
        value = product * scale
        out_ref[0, side * count : (side + 1) * count] = (value + value * jnp.tanh(value)).astype(jnp.bfloat16)


def answers_of(packed, weight, first):
    pairs, count, model = packed[0].shape
    wide = weight.shape[1] // RING
    return pl.pallas_call(
        functools.partial(answers_kernel, 0.5 / math.sqrt(model)),
        grid=(pairs,),
        in_specs=[pl.BlockSpec((1, count, model), lambda i: (i, 0, 0))] * 2
        + [pl.BlockSpec((model, wide), lambda i: (0, first + i))],
        out_specs=pl.BlockSpec((1, 2 * count, wide), lambda i: (i, 0, 0)),
        out_shape=jax.ShapeDtypeStruct((pairs, 2 * count, wide), jnp.bfloat16),
        compiler_params=pltpu.CompilerParams(vmem_limit_bytes=18 * 2**20),
        cost_estimate=pl.CostEstimate(
            flops=4 * pairs * count * model * wide,
            bytes_accessed=4 * pairs * count * (model + wide) + 2 * model * pairs * wide,
            transcendentals=2 * pairs * count * wide,
        ),
    )(*packed, weight)


def unpack_kernel(rows, where_ref, own_ref, other_ref, own_low_ref, own_high_ref, other_low_ref, other_high_ref, out_ref):
    slots = GROUPS * CAP
    tile = GROUPS * rows
    sides = (own_ref, own_low_ref, own_high_ref), (other_ref, other_low_ref, other_high_ref)
    for side, (spread_ref, *answers) in enumerate(sides):
        count = spread_ref.shape[0]
        for part in range(count // tile):
            held = [ref[i, part * slots : (part + 1) * slots] for ref in answers for i in range(2)]
            out = jnp.dot(
                spread_ref[part * tile : (part + 1) * tile],
                jnp.concatenate(held + held),
                preferred_element_type=jnp.float32,
            )
            start = side * count + part * tile
            out_ref[0, start : start + tile] = out.astype(out_ref.dtype)


def unpack(where, spreads, answers, part, rows, dtype):
    blocks = where.shape[0]
    count, wide = spreads[0].shape[0] // RING, spreads[0].shape[1]
    slots, columns = answers[0].shape[1] // (2 * RING), part[1] - part[0]
    column = part[0] // columns
    return pl.pallas_call(
        functools.partial(unpack_kernel, rows),
        grid_spec=pltpu.PrefetchScalarGridSpec(
            num_scalar_prefetch=1,
            grid=(blocks,),
            in_specs=[pl.BlockSpec((count, wide), lambda i, where: (where[i], 0))] * 2
            + [pl.BlockSpec((2, slots, columns), lambda i, where: (0, where[i], column))] * 2
            + [pl.BlockSpec((2, slots, columns), lambda i, where: (0, RING + where[i], column))] * 2,
            out_specs=pl.BlockSpec((1, 2 * count, columns), lambda i, where: (i, 0, 0)),
        ),
        out_shape=jax.ShapeDtypeStruct((blocks, 2 * count, columns), dtype),
        compiler_params=pltpu.CompilerParams(vmem_limit_bytes=18 * 2**20),
        cost_estimate=pl.CostEstimate(
            flops=4 * blocks * count * wide * columns,
            bytes_accessed=4 * blocks * count * (wide + 2 * columns),
            transcendentals=0,
        ),
    )(where, *spreads, *answers, *answers)


def local(deltas, master, momentum, hidden, expert_ids, gate_weights):
    experts, block_rows, width = deltas.shape[1:]
    sub = master.shape[3]
    steps, rows, model = hidden.shape
    top = expert_ids.shape[2]
    z_lo, core = lax.axis_index("z_lo"), lax.axis_index("core")
    y, x, z_hi = lax.axis_index("y"), lax.axis_index("x"), lax.axis_index("z_hi")
    z = z_hi * 2 + z_lo
    taken = steps * rows
    owners = RING * RING
    span = owners * sub
    half_width = width // 2
    cut = 2 * half_width // 3
    parts = [(0, cut), (cut, half_width)]

    pieces = deltas[0].reshape(experts, 2, 2, sub, width)
    kept = lax.dynamic_index_in_dim(pieces, core, axis=2, keepdims=False)
    given = lax.dynamic_index_in_dim(pieces, 1 - core, axis=2, keepdims=False)
    pair = kept.astype(jnp.float32) + swap(given, "core").astype(jnp.float32)
    kept = lax.dynamic_index_in_dim(pair, z_lo, axis=1, keepdims=False)
    given = lax.dynamic_index_in_dim(pair, 1 - z_lo, axis=1, keepdims=False).astype(jnp.bfloat16)
    received = swap(given, "z_lo")
    hidden, expert_ids, gate_weights = [
        later(value, given) for value in (hidden, expert_ids, gate_weights)
    ]

    named = (expert_ids.reshape(taken, top)[:, :, None] == jnp.arange(experts)).astype(jnp.float32)
    row = jnp.arange(taken)
    earlier = (row[:, None] // rows == row // rows) & (row[:, None] > row)
    rank = jnp.dot(
        earlier.astype(jnp.bfloat16),
        jnp.sum(named, axis=1).astype(jnp.bfloat16),
        preferred_element_type=jnp.float32,
    )
    rank = jnp.sum(named * rank[:, None], axis=2).astype(jnp.int32).reshape(expert_ids.shape)
    group = (x % 2) * steps + jnp.arange(steps, dtype=jnp.int32)[:, None, None]
    slot = expert_ids % RING * (GROUPS * CAP) + group * CAP + rank
    gate_high = rounded(gate_weights)
    routing = jnp.concatenate(
        [(expert_ids // RING).astype(jnp.float32), slot.astype(jnp.float32), gate_high, gate_weights - gate_high],
        axis=-1,
    ).astype(jnp.bfloat16)
    routing = jnp.pad(routing.reshape(taken, 4 * top), ((0, 0), (0, LANES - 4 * top)))
    place = jnp.arange(model, dtype=jnp.int32)
    ring_z = (z - 3 + place // (2 * span)) % CHIPS
    source = (place // sub % owners) * RING + ring_z // 2
    source = source * block_rows + (ring_z % 2) * 2 * sub + (place // span % 2) * sub + place % sub
    ordering = (jnp.arange(model, dtype=jnp.int32)[:, None] == source[None, :]).astype(jnp.bfloat16)
    flat = jnp.dot(
        hidden.reshape(taken, model), ordering, preferred_element_type=jnp.float32
    ).astype(jnp.bfloat16)
    flat = jnp.concatenate([flat, routing], axis=1)
    flat = with_layout_constraint(flat, Layout(major_to_minor=(0, 1)))

    plane = lax.all_gather(flat, ("y", "x"), axis=0, tiled=True)
    params = master.reshape(experts, sub, width)
    velocity_old = momentum.reshape(experts, sub, width)
    outer_grad = (kept + received.astype(jnp.float32)) / 4
    velocity = outer_momentum * velocity_old + outer_grad
    piece = (params - outer_rate * (outer_grad + outer_momentum * velocity)).astype(jnp.bfloat16)

    piece = piece.reshape(owners, RING, sub, 2, half_width).transpose(0, 2, 3, 1, 4)
    piece = piece.reshape(owners, sub, 2 * RING * half_width)
    piece = lax.all_to_all(piece, ("y", "x"), split_axis=0, concat_axis=0, tiled=True)
    piece = piece.reshape(span, 2 * RING * half_width)
    mine = lax.dynamic_slice_in_dim(piece, core * RING * half_width, RING * half_width, axis=1)
    other = lax.dynamic_slice_in_dim(piece, (1 - core) * RING * half_width, RING * half_width, axis=1)
    piece = by_core(core, mine, swap(other, "core"), 0)

    def hop(up, down):
        return lax.ppermute(up, Z, UP), lax.ppermute(down, Z, DOWN)

    hops = [(piece, piece)]
    for _ in range(3):
        hops.append(hop(*hops[-1]))
    here = (y * RING + x).reshape(1)
    packed = pack(here, later(plane, *hops[2]), model, top, rows)
    up, down, _ = lax.optimization_barrier((*hops[3], packed[0]))
    low, high = hop(up[:span], down[span:])
    (up1, down1), (up2, down2), (up3, down3) = hops[1:]
    weight = jnp.concatenate([up3, up2, up1, piece, down1, down2, down3, low, high])

    *packed, spread = packed
    packed = [(part, swap(part, "core")) for part in packed]
    spreads = (spread, swap(spread, "core"))

    answers = [answers_of(part, weight, 2 * index) for index, part in enumerate(packed)]
    far_block = ((y + 2) % RING).reshape(1)
    near_blocks = (y + jnp.array([3, 1, 0], jnp.int32)) % RING

    def far_terms(answers, part):
        return unpack(far_block, spreads, answers, part, rows, jnp.bfloat16)[0]

    def near_terms(answers, part):
        return unpack(near_blocks, spreads, answers, part, rows, jnp.float32)

    def to_rows(ringed):
        wide = ringed.shape[1]
        ringed = ringed.reshape(2, RING, taken, wide)
        own, before, after, far = [
            lax.dynamic_index_in_dim(ringed, (x + offset) % RING, axis=1, keepdims=False)
            for offset in (0, 3, 1, 2)
        ]
        received = [
            lax.ppermute(far.astype(jnp.bfloat16), "x", [(i, (i + 2) % RING) for i in range(RING)]),
            lax.ppermute(after.astype(jnp.bfloat16), "x", PLUS),
            lax.ppermute(before.astype(jnp.bfloat16), "x", MINUS),
        ]
        for value in received:
            own = own + value.astype(jnp.float32)
        return own[0], swap(own[1].astype(jnp.bfloat16), "core").astype(jnp.float32)

    far = far_terms(answers, parts[0])
    near = near_terms([answers[0], later(answers[1], far)], parts[0])
    answers = [answers[0], later(answers[1], near)]
    before, after = far_sums(near[0], near[1], far, "y")
    mine_a, other_a = to_rows(near_sums(near[2], before, after, "y"))
    far = far_terms(answers, parts[1])
    near = near_terms([answers[0], later(answers[1], far)], parts[1])
    before, after = far_sums(near[0], near[1], far, "y")
    own = near[2]
    mine_b, other_b = to_rows(near_sums(own, before, after, "y"))

    mine = lax.dynamic_slice_in_dim(weight, z_hi * half_width, half_width, axis=1)
    mine = later(mine, own)
    engine = by_core(core, mine, swap(mine, "core"), 1)
    engine = engine.reshape(CHIPS, 2, owners, sub, width)
    engine = jnp.concatenate([engine, engine])
    engine = lax.dynamic_slice_in_dim(engine, (CHIPS + 3 - z) % CHIPS, CHIPS, axis=0)
    engine = engine.transpose(2, 0, 1, 3, 4).reshape(model, width)

    mine = jnp.concatenate([mine_a, mine_b], axis=1)
    other = jnp.concatenate([other_a, other_b], axis=1)
    decoded = by_core(core, mine, other, 1).reshape(steps, rows, width).astype(jnp.bfloat16)
    return (engine[None], velocity.reshape(momentum.shape), decoded)


def solution(mesh):
    fine = Mesh(
        mesh.devices.reshape(2, 2, RING, RING, RING), ("z_lo", "core", "y", "x", "z_hi")
    )
    rep, ep = ("z_lo", "core"), ("y", "x", "z_hi")
    return jax.shard_map(
        local,
        mesh=fine,
        in_specs=(
            P(rep, None, ep, None),
            P(None, ep, rep, None, None),
            P(None, ep, rep, None, None),
            P(None, rep + ep, None),
            P(None, rep + ep, None),
            P(None, rep + ep, None),
        ),
        out_specs=(
            P(ep, None, None),
            P(None, ep, rep, None, None),
            P(None, rep + ep, None),
        ),
        check_vma=False,
    )
```

```python
import functools
import math

import jax
import jax.numpy as jnp
from jax import lax
from jax.experimental import pallas as pl
from jax.experimental.layout import Layout, with_layout_constraint
from jax.experimental.pallas import tpu as pltpu
from jax.sharding import Mesh, PartitionSpec as P

outer_momentum = 0.9
outer_rate = 0.7

RING = 4
LANES = 128
CAP = 6
GROUPS = 8
PLUS = [(i, (i + 1) % RING) for i in range(RING)]
MINUS = [(i, (i - 1) % RING) for i in range(RING)]
CHIPS = 8
Z = ("z_lo", "z_hi")
UP = [(i % 2 * RING + i // 2, (i + 1) % CHIPS % 2 * RING + (i + 1) % CHIPS // 2) for i in range(CHIPS)]
DOWN = [(after, before) for before, after in UP]
SWAP = [(0, 1), (1, 0)]


def swap(value, axis):
    return lax.ppermute(value, axis, SWAP)


def later(value, *first):
    return lax.optimization_barrier((value,) + first)[0]


def neighbours(value, axis):
    return lax.ppermute(value, axis, PLUS), lax.ppermute(value, axis, MINUS)


def forward(before, after, axis):
    half = before.shape[0] // 2
    low = lax.ppermute(before[:half], axis, PLUS)
    high = lax.ppermute(after[half:], axis, MINUS)
    return jnp.concatenate([low, high])


def far_sums(before, after, far, axis):
    half = far.shape[0] // 2
    low = lax.ppermute(far[:half].astype(jnp.bfloat16), axis, PLUS)
    high = lax.ppermute(far[half:].astype(jnp.bfloat16), axis, MINUS)
    after = jnp.concatenate([after[:half] + low.astype(jnp.float32), after[half:]])
    before = jnp.concatenate([before[:half], before[half:] + high.astype(jnp.float32)])
    return before.astype(jnp.bfloat16), after.astype(jnp.bfloat16)


def near_sums(own, before, after, axis):
    from_before = lax.ppermute(after, axis, PLUS)
    from_after = lax.ppermute(before, axis, MINUS)
    return own + from_before.astype(jnp.float32) + from_after.astype(jnp.float32)


def by_core(core, mine, other, axis):
    return jnp.where(
        core == 0,
        jnp.concatenate([mine, other], axis=axis),
        jnp.concatenate([other, mine], axis=axis),
    )


def rounded(value):
    return lax.reduce_precision(value, exponent_bits=8, mantissa_bits=7)


def pack_kernel(top, where_ref, row_ref, packed_ref, spread_ref):
    count, model, slots = row_ref.shape[0], packed_ref.shape[2], packed_ref.shape[1]
    wide = RING * slots
    routing = row_ref[:, model : model + LANES].astype(jnp.float32)
    place = jnp.where(routing[:, :top] == where_ref[0].astype(jnp.float32), routing[:, top : 2 * top], -wide - 1.0)
    lane = lax.broadcasted_iota(jnp.int32, (count, 2 * wide), 1).astype(jnp.float32)
    spread = jnp.zeros((count, 2 * wide), jnp.float32)
    placed = jnp.zeros((count, wide), jnp.float32)
    for choice in range(top):
        here = place[:, choice : choice + 1]
        high = routing[:, 2 * top + choice : 2 * top + choice + 1]
        rest = routing[:, 3 * top + choice : 3 * top + choice + 1]
        spread = jnp.where(lane == here, high, jnp.where(lane == here + wide, rest, spread))
        placed = jnp.where(lane[:, :wide] == here, 1.0, placed)
    spread_ref[...] = spread.astype(jnp.bfloat16)
    packed = lax.dot_general(
        placed.astype(jnp.bfloat16),
        row_ref[:, :model],
        (((0,), (0,)), ((), ())),
        preferred_element_type=jnp.float32,
    ).astype(jnp.bfloat16)
    for offset in range(RING):
        packed_ref[offset] = packed[offset * slots : (offset + 1) * slots]


def pack(where, plane, model, top, rows):
    count, columns = plane.shape
    tile = GROUPS * rows
    tiles = count // tile
    slots = GROUPS * CAP
    return pl.pallas_call(
        functools.partial(pack_kernel, top),
        grid=(tiles,),
        in_specs=[
            pl.BlockSpec(memory_space=pltpu.SMEM),
            pl.BlockSpec((tile, columns), lambda i: (i, 0)),
        ],
        out_specs=[
            pl.BlockSpec((RING, slots, model), lambda i: (0, i, 0)),
            pl.BlockSpec((tile, 2 * RING * slots), lambda i: (i, 0)),
        ],
        out_shape=[
            jax.ShapeDtypeStruct((RING, tiles * slots, model), jnp.bfloat16),
            jax.ShapeDtypeStruct((count, 2 * RING * slots), jnp.bfloat16),
        ],
        compiler_params=pltpu.CompilerParams(vmem_limit_bytes=48 * 2**20),
        cost_estimate=pl.CostEstimate(
            flops=2 * count * RING * slots * model,
            bytes_accessed=2 * count * columns + 2 * tiles * slots * RING * model,
            transcendentals=0,
        ),
    )(where, plane)


def passed_on(values, first):
    anywhere = pl.BlockSpec(memory_space=pl.ANY)
    count = len(values)
    return pl.pallas_call(
        lambda *refs: None,
        in_specs=[anywhere] * (count + 1),
        out_specs=[anywhere] * count,
        out_shape=[jax.ShapeDtypeStruct(value.shape, value.dtype) for value in values],
        input_output_aliases={index: index for index in range(count)},
        compiler_params=pltpu.CompilerParams(vmem_limit_bytes=2**20),
    )(*values, first)


def answers_kernel(scale, which_ref, packed_ref, *refs):
    *pieces, out_ref, served_ref, weight_ref = refs
    start = 0
    for piece in pieces:
        weight_ref[start : start + piece.shape[0]] = piece[...]
        start += piece.shape[0]
    product = jnp.dot(packed_ref[0], weight_ref[...], preferred_element_type=jnp.float32)
    value = product * scale
    out_ref[0] = (value + value * jnp.tanh(value)).astype(jnp.bfloat16)

    @pl.when(pl.program_id(0) == which_ref[0])
    def _():
        served_ref[...] = weight_ref[...]


def answers_of(which, packed, pieces):
    _, count, model = packed.shape
    wide = pieces[0].shape[1] // RING
    return pl.pallas_call(
        functools.partial(answers_kernel, 0.5 / math.sqrt(model)),
        grid=(RING,),
        in_specs=[
            pl.BlockSpec(memory_space=pltpu.SMEM),
            pl.BlockSpec((1, count, model), lambda i: (i, 0, 0)),
        ]
        + [pl.BlockSpec((piece.shape[0], wide), lambda i: (0, i)) for piece in pieces],
        out_specs=[
            pl.BlockSpec((1, count, wide), lambda i: (i, 0, 0)),
            pl.BlockSpec((model, wide), lambda i: (0, 0)),
        ],
        out_shape=[
            jax.ShapeDtypeStruct((RING, count, wide), jnp.bfloat16),
            jax.ShapeDtypeStruct((model, wide), jnp.bfloat16),
        ],
        scratch_shapes=[pltpu.VMEM((model, wide), jnp.bfloat16)],
        compiler_params=pltpu.CompilerParams(vmem_limit_bytes=32 * 2**20),
        cost_estimate=pl.CostEstimate(
            flops=2 * RING * count * model * wide,
            bytes_accessed=2 * RING * (count * (model + wide) + model * wide),
            transcendentals=RING * count * wide,
        ),
    )(which, packed, *pieces)


def unpack_kernel(rows, where_ref, spread_ref, answers_ref, first_ref, out_ref):
    slots = GROUPS * CAP
    tile = GROUPS * rows
    for start in range(0, spread_ref.shape[0], tile):
        part = start // tile * slots
        held = [answers_ref[i, part : part + slots] for i in range(RING)]
        out = jnp.dot(
            spread_ref[start : start + tile],
            jnp.concatenate(held + held),
            preferred_element_type=jnp.float32,
        )
        out_ref[0, start : start + tile] = out.astype(out_ref.dtype)


def unpack(where, spread, answers, part, rows, dtype, first):
    blocks = where.shape[0]
    count, wide = spread.shape[0] // RING, spread.shape[1]
    slots, columns = answers.shape[1] // RING, part[1] - part[0]
    column = part[0] // columns
    return pl.pallas_call(
        functools.partial(unpack_kernel, rows),
        grid_spec=pltpu.PrefetchScalarGridSpec(
            num_scalar_prefetch=1,
            grid=(blocks,),
            in_specs=[
                pl.BlockSpec((count, wide), lambda i, where: (where[i], 0)),
                pl.BlockSpec((RING, slots, columns), lambda i, where: (0, where[i], column)),
                pl.BlockSpec(memory_space=pl.ANY),
            ],
            out_specs=pl.BlockSpec((1, count, columns), lambda i, where: (i, 0, 0)),
        ),
        out_shape=jax.ShapeDtypeStruct((blocks, count, columns), dtype),
        compiler_params=pltpu.CompilerParams(vmem_limit_bytes=18 * 2**20),
        cost_estimate=pl.CostEstimate(
            flops=2 * blocks * count * wide * columns,
            bytes_accessed=2 * blocks * count * (wide + 2 * columns),
            transcendentals=0,
        ),
    )(where, spread, answers, first)


def local(deltas, master, momentum, hidden, expert_ids, gate_weights):
    experts, block_rows, width = deltas.shape[1:]
    sub = master.shape[3]
    steps, rows, model = hidden.shape
    top = expert_ids.shape[2]
    z_lo, core = lax.axis_index("z_lo"), lax.axis_index("core")
    y, x, z_hi = lax.axis_index("y"), lax.axis_index("x"), lax.axis_index("z_hi")
    z = z_hi * 2 + z_lo
    taken = steps * rows
    owners = RING * RING
    span = owners * sub
    cut = 2 * width // 3
    parts = [(0, cut), (cut, width)]

    pieces = deltas[0].reshape(experts, 2, 2, sub, width)
    kept = lax.dynamic_index_in_dim(pieces, core, axis=2, keepdims=False)
    given = lax.dynamic_index_in_dim(pieces, 1 - core, axis=2, keepdims=False)
    other = swap(given, "core")

    def pair(index):
        both = [lax.dynamic_index_in_dim(value, index, axis=1, keepdims=False) for value in (kept, other)]
        return both[0].astype(jnp.float32) + both[1].astype(jnp.float32)

    given = pair(1 - z_lo).astype(jnp.bfloat16)
    received = swap(given, "z_lo")
    hidden, expert_ids, gate_weights = [
        later(value, given) for value in (hidden, expert_ids, gate_weights)
    ]

    named = (expert_ids.reshape(taken, top)[:, :, None] == jnp.arange(experts)).astype(jnp.float32)
    row = jnp.arange(taken)
    earlier = (row[:, None] // rows == row // rows) & (row[:, None] > row)
    rank = jnp.dot(
        earlier.astype(jnp.bfloat16),
        jnp.sum(named, axis=1).astype(jnp.bfloat16),
        preferred_element_type=jnp.float32,
    )
    rank = jnp.sum(named * rank[:, None], axis=2).astype(jnp.int32).reshape(expert_ids.shape)
    group = (x % 2) * steps + jnp.arange(steps, dtype=jnp.int32)[:, None, None]
    slot = expert_ids % RING * (GROUPS * CAP) + group * CAP + rank
    gate_high = rounded(gate_weights)
    routing = jnp.concatenate(
        [(expert_ids // RING).astype(jnp.float32), slot.astype(jnp.float32), gate_high, gate_weights - gate_high],
        axis=-1,
    ).astype(jnp.bfloat16)
    routing = jnp.pad(routing.reshape(taken, 4 * top), ((0, 0), (0, LANES - 4 * top)))
    place = jnp.arange(model, dtype=jnp.int32)
    turn = place // span % CHIPS
    ring_z = z + jnp.where(turn < 3, turn - 1, jnp.where(turn % 2 == 1, -1, 1) * (turn // 2 + turn % 2))
    ring_z = (z + jnp.where(turn == 7, 4, ring_z - z)) % CHIPS
    ring_core = (core + place // (CHIPS * span)) % 2
    source = (place // sub % owners) * RING + ring_z // 2
    source = source * block_rows + (ring_z % 2) * 2 * sub + ring_core * sub + place % sub
    ordering = (jnp.arange(model, dtype=jnp.int32)[:, None] == source[None, :]).astype(jnp.bfloat16)
    flat = jnp.dot(
        hidden.reshape(taken, model), ordering, preferred_element_type=jnp.float32
    ).astype(jnp.bfloat16)
    flat = jnp.concatenate([flat, routing], axis=1)
    flat = with_layout_constraint(flat, Layout(major_to_minor=(0, 1)))

    plane = lax.all_gather(flat, ("y", "x"), axis=0, tiled=True)
    params = master.reshape(experts, sub, width)
    velocity_old = momentum.reshape(experts, sub, width)
    outer_grad = (pair(z_lo) + received.astype(jnp.float32)) / 4
    velocity = outer_momentum * velocity_old + outer_grad
    piece = (params - outer_rate * (outer_grad + outer_momentum * velocity)).astype(jnp.bfloat16)

    piece = piece.reshape(owners, RING, sub, width).transpose(0, 2, 1, 3).reshape(owners, sub, RING * width)
    piece = lax.all_to_all(piece, ("y", "x"), split_axis=0, concat_axis=0, tiled=True)
    piece = piece.reshape(span, RING * width)

    def hop(up, down):
        return lax.ppermute(up, Z, UP), lax.ppermute(down, Z, DOWN)

    hops = [(piece, piece)]
    for _ in range(3):
        hops.append(hop(*hops[-1]))
    here = (y * RING + x).reshape(1)
    packed, spread = pack(here, plane, model, top, rows)
    up, down = passed_on(hops[3], spread)
    low, high = hop(up[: span // 2], down[span // 2 :])
    (up1, down1), (up2, down2) = hops[1:3]
    first = [up1, piece, down1]
    rest = [up2, down2, up, down, low, high]
    pieces = first + rest + [swap(jnp.concatenate(first), "core")] + [swap(part, "core") for part in rest]
    answers, engine = answers_of(z_hi.reshape(1), packed, pieces)
    far_block = ((y + 2) % RING).reshape(1)
    near_blocks = (y + jnp.array([3, 1, 0], jnp.int32)) % RING

    def to_rows(ringed):
        ringed = ringed.reshape(RING, taken, -1)
        own, before, after, far = [
            lax.dynamic_index_in_dim(ringed, (x + offset) % RING, axis=0, keepdims=False)
            for offset in (0, 3, 1, 2)
        ]
        received = [
            lax.ppermute(far.astype(jnp.bfloat16), "x", [(i, (i + 2) % RING) for i in range(RING)]),
            lax.ppermute(after.astype(jnp.bfloat16), "x", PLUS),
            lax.ppermute(before.astype(jnp.bfloat16), "x", MINUS),
        ]
        for value in received:
            own = own + value.astype(jnp.float32)
        return own

    first = spread
    decoded = []
    for part in parts:
        far = first = unpack(far_block, spread, answers, part, rows, jnp.bfloat16, first)
        near = first = unpack(near_blocks, spread, answers, part, rows, jnp.float32, first)
        before, after = far_sums(near[0], near[1], far[0], "y")
        decoded.append(to_rows(near_sums(near[2], before, after, "y")))
    decoded = jnp.concatenate(decoded, axis=1).reshape(steps, rows, width).astype(jnp.bfloat16)

    engine = later(engine, near).reshape(2, CHIPS, owners, sub, width)
    engine = by_core(core, engine[:1], engine[1:], 0)
    engine = jnp.concatenate([engine[:, i : i + 1] for i in (5, 3, 0, 1, 2, 4, 6, 7)] * 2, axis=1)
    engine = lax.dynamic_slice_in_dim(engine, (CHIPS + 3 - z) % CHIPS, CHIPS, axis=1)
    engine = engine.transpose(2, 1, 0, 3, 4).reshape(model, width)
    return (engine[None], velocity.reshape(momentum.shape), decoded)


def solution(mesh):
    fine = Mesh(
        mesh.devices.reshape(2, 2, RING, RING, RING), ("z_lo", "core", "y", "x", "z_hi")
    )
    rep, ep = ("z_lo", "core"), ("y", "x", "z_hi")
    return jax.shard_map(
        local,
        mesh=fine,
        in_specs=(
            P(rep, None, ep, None),
            P(None, ep, rep, None, None),
            P(None, ep, rep, None, None),
            P(None, rep + ep, None),
            P(None, rep + ep, None),
            P(None, rep + ep, None),
        ),
        out_specs=(
            P(ep, None, None),
            P(None, ep, rep, None, None),
            P(None, rep + ep, None),
        ),
        check_vma=False,
    )
```

```python
import functools
import math

import jax
import jax.numpy as jnp
from jax import lax
from jax.experimental import pallas as pl
from jax.experimental.layout import Layout, with_layout_constraint
from jax.experimental.pallas import tpu as pltpu
from jax.sharding import Mesh, PartitionSpec as P

outer_momentum = 0.9
outer_rate = 0.7

RING = 4
LANES = 128
CAP = 6
GROUPS = 8
PLUS = [(i, (i + 1) % RING) for i in range(RING)]
MINUS = [(i, (i - 1) % RING) for i in range(RING)]
CHIPS = 8
Z = ("z_lo", "z_hi")
UP = [(i % 2 * RING + i // 2, (i + 1) % CHIPS % 2 * RING + (i + 1) % CHIPS // 2) for i in range(CHIPS)]
DOWN = [(after, before) for before, after in UP]
SWAP = [(0, 1), (1, 0)]


def swap(value, axis):
    return lax.ppermute(value, axis, SWAP)


def later(value, *first):
    return lax.optimization_barrier((value,) + first)[0]


def neighbours(value, axis):
    return lax.ppermute(value, axis, PLUS), lax.ppermute(value, axis, MINUS)


def forward(before, after, axis):
    half = before.shape[0] // 2
    low = lax.ppermute(before[:half], axis, PLUS)
    high = lax.ppermute(after[half:], axis, MINUS)
    return jnp.concatenate([low, high])


def far_sums(before, after, far, axis):
    half = far.shape[0] // 2
    low = lax.ppermute(far[:half].astype(jnp.bfloat16), axis, PLUS)
    high = lax.ppermute(far[half:].astype(jnp.bfloat16), axis, MINUS)
    after = jnp.concatenate([after[:half] + low.astype(jnp.float32), after[half:]])
    before = jnp.concatenate([before[:half], before[half:] + high.astype(jnp.float32)])
    return before.astype(jnp.bfloat16), after.astype(jnp.bfloat16)


def near_sums(own, before, after, axis):
    from_before = lax.ppermute(after, axis, PLUS)
    from_after = lax.ppermute(before, axis, MINUS)
    return own + from_before.astype(jnp.float32) + from_after.astype(jnp.float32)


def by_core(core, mine, other, axis):
    return jnp.where(
        core == 0,
        jnp.concatenate([mine, other], axis=axis),
        jnp.concatenate([other, mine], axis=axis),
    )


def rounded(value):
    return lax.reduce_precision(value, exponent_bits=8, mantissa_bits=7)


def pack_kernel(top, where_ref, row_ref, packed_ref, spread_ref):
    count, model, slots = row_ref.shape[0], packed_ref.shape[2], packed_ref.shape[1]
    wide = RING * slots
    routing = row_ref[:, model : model + LANES].astype(jnp.float32)
    place = jnp.where(routing[:, :top] == where_ref[0].astype(jnp.float32), routing[:, top : 2 * top], -wide - 1.0)
    lane = lax.broadcasted_iota(jnp.int32, (count, 2 * wide), 1).astype(jnp.float32)
    spread = jnp.zeros((count, 2 * wide), jnp.float32)
    placed = jnp.zeros((count, wide), jnp.float32)
    for choice in range(top):
        here = place[:, choice : choice + 1]
        high = routing[:, 2 * top + choice : 2 * top + choice + 1]
        rest = routing[:, 3 * top + choice : 3 * top + choice + 1]
        spread = jnp.where(lane == here, high, jnp.where(lane == here + wide, rest, spread))
        placed = jnp.where(lane[:, :wide] == here, 1.0, placed)
    spread_ref[...] = spread.astype(jnp.bfloat16)
    packed = lax.dot_general(
        placed.astype(jnp.bfloat16),
        row_ref[:, :model],
        (((0,), (0,)), ((), ())),
        preferred_element_type=jnp.float32,
    ).astype(jnp.bfloat16)
    for offset in range(RING):
        packed_ref[offset] = packed[offset * slots : (offset + 1) * slots]


def pack(where, plane, model, top, rows):
    count, columns = plane.shape
    tile = GROUPS * rows
    tiles = count // tile
    slots = GROUPS * CAP
    return pl.pallas_call(
        functools.partial(pack_kernel, top),
        grid=(tiles,),
        in_specs=[
            pl.BlockSpec(memory_space=pltpu.SMEM),
            pl.BlockSpec((tile, columns), lambda i: (i, 0)),
        ],
        out_specs=[
            pl.BlockSpec((RING, slots, model), lambda i: (0, i, 0)),
            pl.BlockSpec((tile, 2 * RING * slots), lambda i: (i, 0)),
        ],
        out_shape=[
            jax.ShapeDtypeStruct((RING, tiles * slots, model), jnp.bfloat16),
            jax.ShapeDtypeStruct((count, 2 * RING * slots), jnp.bfloat16),
        ],
        compiler_params=pltpu.CompilerParams(vmem_limit_bytes=48 * 2**20),
        cost_estimate=pl.CostEstimate(
            flops=2 * count * RING * slots * model,
            bytes_accessed=2 * count * columns + 2 * tiles * slots * RING * model,
            transcendentals=0,
        ),
    )(where, plane)


def passed_on(values, first):
    anywhere = pl.BlockSpec(memory_space=pl.ANY)
    count = len(values)
    return pl.pallas_call(
        lambda *refs: None,
        in_specs=[anywhere] * (count + 1),
        out_specs=[anywhere] * count,
        out_shape=[jax.ShapeDtypeStruct(value.shape, value.dtype) for value in values],
        input_output_aliases={index: index for index in range(count)},
        compiler_params=pltpu.CompilerParams(vmem_limit_bytes=2**20),
    )(*values, first)


def answers_kernel(scale, which_ref, packed_ref, *refs):
    *pieces, out_ref, served_ref, weight_ref = refs
    start = 0
    for piece in pieces:
        weight_ref[start : start + piece.shape[0]] = piece[...]
        start += piece.shape[0]
    product = jnp.dot(packed_ref[0], weight_ref[...], preferred_element_type=jnp.float32)
    value = product * scale
    out_ref[0] = (value + value * jnp.tanh(value)).astype(jnp.bfloat16)

    @pl.when(pl.program_id(0) == which_ref[0])
    def _():
        served_ref[...] = weight_ref[...]


def answers_of(which, packed, pieces):
    _, count, model = packed.shape
    wide = pieces[0].shape[1] // RING
    return pl.pallas_call(
        functools.partial(answers_kernel, 0.5 / math.sqrt(model)),
        grid=(RING,),
        in_specs=[
            pl.BlockSpec(memory_space=pltpu.SMEM),
            pl.BlockSpec((1, count, model), lambda i: (i, 0, 0)),
        ]
        + [pl.BlockSpec((piece.shape[0], wide), lambda i: (0, i)) for piece in pieces],
        out_specs=[
            pl.BlockSpec((1, count, wide), lambda i: (i, 0, 0)),
            pl.BlockSpec((model, wide), lambda i: (0, 0)),
        ],
        out_shape=[
            jax.ShapeDtypeStruct((RING, count, wide), jnp.bfloat16),
            jax.ShapeDtypeStruct((model, wide), jnp.bfloat16),
        ],
        scratch_shapes=[pltpu.VMEM((model, wide), jnp.bfloat16)],
        compiler_params=pltpu.CompilerParams(vmem_limit_bytes=32 * 2**20),
        cost_estimate=pl.CostEstimate(
            flops=2 * RING * count * model * wide,
            bytes_accessed=2 * RING * (count * (model + wide) + model * wide),
            transcendentals=RING * count * wide,
        ),
    )(which, packed, *pieces)


def unpack_kernel(rows, where_ref, spread_ref, answers_ref, first_ref, out_ref):
    slots = GROUPS * CAP
    tile = min(GROUPS * rows, spread_ref.shape[0])
    for start in range(0, spread_ref.shape[0], tile):
        part = start // tile * slots
        held = [answers_ref[i, part : part + slots] for i in range(RING)]
        out = jnp.dot(
            spread_ref[start : start + tile],
            jnp.concatenate(held + held),
            preferred_element_type=jnp.float32,
        )
        out_ref[0, start : start + tile] = out.astype(out_ref.dtype)


def unpack(where, spread, answers, part, axis, rows, dtype, first):
    blocks = where.shape[0]
    count, wide = spread.shape[0] // RING, spread.shape[1]
    slots, columns = answers.shape[1] // RING, part[1] - part[0]
    column = part[0] // columns
    if axis == "y":
        grid = (blocks, 1)
        spread_spec = pl.BlockSpec((count, wide), lambda i, j, where: (where[i], 0))
        answers_spec = pl.BlockSpec((RING, slots, columns), lambda i, j, where: (0, where[i], column))
        out_spec = pl.BlockSpec((1, count, columns), lambda i, j, where: (i, 0, 0))
    else:
        grid = (blocks, RING)
        spread_spec = pl.BlockSpec((count // RING, wide), lambda i, j, where: (j * RING + where[i], 0))
        answers_spec = pl.BlockSpec(
            (RING, slots // 2, columns), lambda i, j, where: (0, j * 2 + where[i] // 2, column)
        )
        out_spec = pl.BlockSpec((1, count // RING, columns), lambda i, j, where: (i, j, 0))
    return pl.pallas_call(
        functools.partial(unpack_kernel, rows),
        grid_spec=pltpu.PrefetchScalarGridSpec(
            num_scalar_prefetch=1,
            grid=grid,
            in_specs=[spread_spec, answers_spec, pl.BlockSpec(memory_space=pl.ANY)],
            out_specs=out_spec,
        ),
        out_shape=jax.ShapeDtypeStruct((blocks, count, columns), dtype),
        compiler_params=pltpu.CompilerParams(vmem_limit_bytes=18 * 2**20),
        cost_estimate=pl.CostEstimate(
            flops=2 * blocks * count * wide * columns,
            bytes_accessed=2 * blocks * count * (wide + 2 * columns),
            transcendentals=0,
        ),
    )(where, spread, answers, first)


def local(deltas, master, momentum, hidden, expert_ids, gate_weights):
    experts, block_rows, width = deltas.shape[1:]
    sub = master.shape[3]
    steps, rows, model = hidden.shape
    top = expert_ids.shape[2]
    z_lo, core = lax.axis_index("z_lo"), lax.axis_index("core")
    y, x, z_hi = lax.axis_index("y"), lax.axis_index("x"), lax.axis_index("z_hi")
    z = z_hi * 2 + z_lo
    taken = steps * rows
    owners = RING * RING
    span = owners * sub
    cut = width // 2

    pieces = deltas[0].reshape(experts, 2, 2, sub, width)
    kept = lax.dynamic_index_in_dim(pieces, core, axis=2, keepdims=False)
    given = lax.dynamic_index_in_dim(pieces, 1 - core, axis=2, keepdims=False)
    other = swap(given, "core")

    def pair(index):
        both = [lax.dynamic_index_in_dim(value, index, axis=1, keepdims=False) for value in (kept, other)]
        return both[0].astype(jnp.float32) + both[1].astype(jnp.float32)

    given = pair(1 - z_lo).astype(jnp.bfloat16)
    received = swap(given, "z_lo")
    hidden, expert_ids, gate_weights = [
        later(value, given) for value in (hidden, expert_ids, gate_weights)
    ]

    named = (expert_ids.reshape(taken, top)[:, :, None] == jnp.arange(experts)).astype(jnp.float32)
    row = jnp.arange(taken)
    earlier = (row[:, None] // rows == row // rows) & (row[:, None] > row)
    rank = jnp.dot(
        earlier.astype(jnp.bfloat16),
        jnp.sum(named, axis=1).astype(jnp.bfloat16),
        preferred_element_type=jnp.float32,
    )
    rank = jnp.sum(named * rank[:, None], axis=2).astype(jnp.int32).reshape(expert_ids.shape)
    group = (x % 2) * steps + jnp.arange(steps, dtype=jnp.int32)[:, None, None]
    slot = expert_ids % RING * (GROUPS * CAP) + group * CAP + rank
    gate_high = rounded(gate_weights)
    routing = jnp.concatenate(
        [(expert_ids // RING).astype(jnp.float32), slot.astype(jnp.float32), gate_high, gate_weights - gate_high],
        axis=-1,
    ).astype(jnp.bfloat16)
    routing = jnp.pad(routing.reshape(taken, 4 * top), ((0, 0), (0, LANES - 4 * top)))
    place = jnp.arange(model, dtype=jnp.int32)
    turn = place // span % CHIPS
    ring_z = z + jnp.where(turn < 3, turn - 1, jnp.where(turn % 2 == 1, -1, 1) * (turn // 2 + turn % 2))
    ring_z = (z + jnp.where(turn == 7, 4, ring_z - z)) % CHIPS
    ring_core = (core + place // (CHIPS * span)) % 2
    source = (place // sub % owners) * RING + ring_z // 2
    source = source * block_rows + (ring_z % 2) * 2 * sub + ring_core * sub + place % sub
    ordering = (jnp.arange(model, dtype=jnp.int32)[:, None] == source[None, :]).astype(jnp.bfloat16)
    flat = jnp.dot(
        hidden.reshape(taken, model), ordering, preferred_element_type=jnp.float32
    ).astype(jnp.bfloat16)
    flat = jnp.concatenate([flat, routing], axis=1)
    flat = with_layout_constraint(flat, Layout(major_to_minor=(0, 1)))

    plane = lax.all_gather(flat, ("y", "x"), axis=0, tiled=True)
    params = master.reshape(experts, sub, width)
    velocity_old = momentum.reshape(experts, sub, width)
    outer_grad = (pair(z_lo) + received.astype(jnp.float32)) / 4
    velocity = outer_momentum * velocity_old + outer_grad
    piece = (params - outer_rate * (outer_grad + outer_momentum * velocity)).astype(jnp.bfloat16)

    piece = piece.reshape(owners, RING, sub, width).transpose(0, 2, 1, 3).reshape(owners, sub, RING * width)
    piece = lax.all_to_all(piece, ("y", "x"), split_axis=0, concat_axis=0, tiled=True)
    piece = piece.reshape(span, RING * width)

    def hop(up, down):
        return lax.ppermute(up, Z, UP), lax.ppermute(down, Z, DOWN)

    hops = [(piece, piece)]
    for _ in range(3):
        hops.append(hop(*hops[-1]))
    here = (y * RING + x).reshape(1)
    packed, spread = pack(here, plane, model, top, rows)
    up, down = passed_on(hops[3], spread)
    low, high = hop(up[: span // 2], down[span // 2 :])
    (up1, down1), (up2, down2) = hops[1:3]
    first = [up1, piece, down1]
    rest = [up2, down2, up, down, low, high]
    pieces = first + rest + [swap(jnp.concatenate(first), "core")] + [swap(part, "core") for part in rest]
    answers, engine = answers_of(z_hi.reshape(1), packed, pieces)

    def last_ring(summed, axis, at):
        summed = summed.reshape(RING, taken, -1)
        own, before, after, far = [
            lax.dynamic_index_in_dim(summed, (at + offset) % RING, axis=0, keepdims=False)
            for offset in (0, 3, 1, 2)
        ]
        received = [
            lax.ppermute(far.astype(jnp.bfloat16), axis, [(i, (i + 2) % RING) for i in range(RING)]),
            lax.ppermute(after.astype(jnp.bfloat16), axis, PLUS),
            lax.ppermute(before.astype(jnp.bfloat16), axis, MINUS),
        ]
        for value in received:
            own = own + value.astype(jnp.float32)
        return own

    ways = [((0, cut), "y", y, "x", x), ((cut, width), "x", x, "y", y)]
    first = spread
    fars, nears, decoded = [], [], []
    for part, axis, at, _, _ in ways:
        block = ((at + 2) % RING).reshape(1)
        first = unpack(block, spread, answers, part, axis, rows, jnp.bfloat16, first)
        fars.append(first)
    for part, axis, at, _, _ in ways:
        near_blocks = (at + jnp.array([3, 1, 0], jnp.int32)) % RING
        first = unpack(near_blocks, spread, answers, part, axis, rows, jnp.float32, first)
        nears.append(first)
    for far, terms, (_, axis, _, second, at) in zip(fars, nears, ways):
        before, after = far_sums(terms[0], terms[1], far[0], axis)
        decoded.append(last_ring(near_sums(terms[2], before, after, axis), second, at))
    (engine,) = passed_on([engine], before)
    decoded = jnp.concatenate(decoded, axis=1).reshape(steps, rows, width).astype(jnp.bfloat16)

    engine = engine.reshape(2, CHIPS, owners, sub, width)
    engine = by_core(core, engine[:1], engine[1:], 0)
    engine = jnp.concatenate([engine[:, i : i + 1] for i in (5, 3, 0, 1, 2, 4, 6, 7)] * 2, axis=1)
    engine = lax.dynamic_slice_in_dim(engine, (CHIPS + 3 - z) % CHIPS, CHIPS, axis=1)
    engine = engine.transpose(2, 1, 0, 3, 4).reshape(model, width)
    return (engine[None], velocity.reshape(momentum.shape), decoded)


def solution(mesh):
    fine = Mesh(
        mesh.devices.reshape(2, 2, RING, RING, RING), ("z_lo", "core", "y", "x", "z_hi")
    )
    rep, ep = ("z_lo", "core"), ("y", "x", "z_hi")
    return jax.shard_map(
        local,
        mesh=fine,
        in_specs=(
            P(rep, None, ep, None),
            P(None, ep, rep, None, None),
            P(None, ep, rep, None, None),
            P(None, rep + ep, None),
            P(None, rep + ep, None),
            P(None, rep + ep, None),
        ),
        out_specs=(
            P(ep, None, None),
            P(None, ep, rep, None, None),
            P(None, rep + ep, None),
        ),
        check_vma=False,
    )
```

```python
import functools
import math

import jax
import jax.numpy as jnp
from jax import lax
from jax.experimental import pallas as pl
from jax.experimental.layout import Layout, with_layout_constraint
from jax.experimental.pallas import tpu as pltpu
from jax.sharding import Mesh, PartitionSpec as P

outer_momentum = 0.9
outer_rate = 0.7

RING = 4
LANES = 128
CAP = 6
GROUPS = 8
PLUS = [(i, (i + 1) % RING) for i in range(RING)]
MINUS = [(i, (i - 1) % RING) for i in range(RING)]
CHIPS = 8
Z = ("z_lo", "z_hi")
UP = [(i % 2 * RING + i // 2, (i + 1) % CHIPS % 2 * RING + (i + 1) % CHIPS // 2) for i in range(CHIPS)]
DOWN = [(after, before) for before, after in UP]
SWAP = [(0, 1), (1, 0)]


def swap(value, axis):
    return lax.ppermute(value, axis, SWAP)


def later(value, *first):
    return lax.optimization_barrier((value,) + first)[0]


def neighbours(value, axis):
    return lax.ppermute(value, axis, PLUS), lax.ppermute(value, axis, MINUS)


def forward(before, after, axis):
    half = before.shape[0] // 2
    low = lax.ppermute(before[:half], axis, PLUS)
    high = lax.ppermute(after[half:], axis, MINUS)
    return jnp.concatenate([low, high])


def far_sums(before, after, far, axis):
    half = far.shape[0] // 2
    low = lax.ppermute(far[:half].astype(jnp.bfloat16), axis, PLUS)
    high = lax.ppermute(far[half:].astype(jnp.bfloat16), axis, MINUS)
    after = jnp.concatenate([after[:half] + low.astype(jnp.float32), after[half:]])
    before = jnp.concatenate([before[:half], before[half:] + high.astype(jnp.float32)])
    return before.astype(jnp.bfloat16), after.astype(jnp.bfloat16)


def near_sums(own, before, after, axis):
    from_before = lax.ppermute(after, axis, PLUS)
    from_after = lax.ppermute(before, axis, MINUS)
    return own + from_before.astype(jnp.float32) + from_after.astype(jnp.float32)


def by_core(core, mine, other, axis):
    return jnp.where(
        core == 0,
        jnp.concatenate([mine, other], axis=axis),
        jnp.concatenate([other, mine], axis=axis),
    )


def rounded(value):
    return lax.reduce_precision(value, exponent_bits=8, mantissa_bits=7)


def pack_kernel(top, where_ref, row_ref, packed_ref, spread_ref):
    count, model, slots = row_ref.shape[0], packed_ref.shape[2], packed_ref.shape[1]
    wide = RING * slots
    routing = row_ref[:, model : model + LANES].astype(jnp.float32)
    place = jnp.where(routing[:, :top] == where_ref[0].astype(jnp.float32), routing[:, top : 2 * top], -wide - 1.0)
    lane = lax.broadcasted_iota(jnp.int32, (count, 2 * wide), 1).astype(jnp.float32)
    spread = jnp.zeros((count, 2 * wide), jnp.float32)
    placed = jnp.zeros((count, wide), jnp.float32)
    for choice in range(top):
        here = place[:, choice : choice + 1]
        high = routing[:, 2 * top + choice : 2 * top + choice + 1]
        rest = routing[:, 3 * top + choice : 3 * top + choice + 1]
        spread = jnp.where(lane == here, high, jnp.where(lane == here + wide, rest, spread))
        placed = jnp.where(lane[:, :wide] == here, 1.0, placed)
    spread_ref[...] = spread.astype(jnp.bfloat16)
    packed = lax.dot_general(
        placed.astype(jnp.bfloat16),
        row_ref[:, :model],
        (((0,), (0,)), ((), ())),
        preferred_element_type=jnp.float32,
    ).astype(jnp.bfloat16)
    for offset in range(RING):
        packed_ref[offset] = packed[offset * slots : (offset + 1) * slots]


def pack(where, plane, model, top, rows):
    count, columns = plane.shape
    tile = GROUPS * rows
    tiles = count // tile
    slots = GROUPS * CAP
    return pl.pallas_call(
        functools.partial(pack_kernel, top),
        grid=(tiles,),
        in_specs=[
            pl.BlockSpec(memory_space=pltpu.SMEM),
            pl.BlockSpec((tile, columns), lambda i: (i, 0)),
        ],
        out_specs=[
            pl.BlockSpec((RING, slots, model), lambda i: (0, i, 0)),
            pl.BlockSpec((tile, 2 * RING * slots), lambda i: (i, 0)),
        ],
        out_shape=[
            jax.ShapeDtypeStruct((RING, tiles * slots, model), jnp.bfloat16),
            jax.ShapeDtypeStruct((count, 2 * RING * slots), jnp.bfloat16),
        ],
        compiler_params=pltpu.CompilerParams(vmem_limit_bytes=48 * 2**20),
        cost_estimate=pl.CostEstimate(
            flops=2 * count * RING * slots * model,
            bytes_accessed=2 * count * columns + 2 * tiles * slots * RING * model,
            transcendentals=0,
        ),
    )(where, plane)


def passed_on(values, first):
    anywhere = pl.BlockSpec(memory_space=pl.ANY)
    count = len(values)
    return pl.pallas_call(
        lambda *refs: None,
        in_specs=[anywhere] * (count + 1),
        out_specs=[anywhere] * count,
        out_shape=[jax.ShapeDtypeStruct(value.shape, value.dtype) for value in values],
        input_output_aliases={index: index for index in range(count)},
        compiler_params=pltpu.CompilerParams(vmem_limit_bytes=2**20),
    )(*values, first)


def answers_kernel(scale, which_ref, packed_ref, *refs):
    *pieces, out_ref, served_ref, weight_ref = refs
    start = 0
    for piece in pieces:
        weight_ref[start : start + piece.shape[0]] = piece[...]
        start += piece.shape[0]
    product = jnp.dot(packed_ref[0], weight_ref[...], preferred_element_type=jnp.float32)
    value = product * scale
    out_ref[0] = (value + value * jnp.tanh(value)).astype(jnp.bfloat16)

    @pl.when(pl.program_id(0) == which_ref[0])
    def _():
        served_ref[...] = weight_ref[...]


def answers_of(which, packed, pieces):
    _, count, model = packed.shape
    wide = pieces[0].shape[1] // RING
    return pl.pallas_call(
        functools.partial(answers_kernel, 0.5 / math.sqrt(model)),
        grid=(RING,),
        in_specs=[
            pl.BlockSpec(memory_space=pltpu.SMEM),
            pl.BlockSpec((1, count, model), lambda i: (i, 0, 0)),
        ]
        + [pl.BlockSpec((piece.shape[0], wide), lambda i: (0, i)) for piece in pieces],
        out_specs=[
            pl.BlockSpec((1, count, wide), lambda i: (i, 0, 0)),
            pl.BlockSpec((model, wide), lambda i: (0, 0)),
        ],
        out_shape=[
            jax.ShapeDtypeStruct((RING, count, wide), jnp.bfloat16),
            jax.ShapeDtypeStruct((model, wide), jnp.bfloat16),
        ],
        scratch_shapes=[pltpu.VMEM((model, wide), jnp.bfloat16)],
        compiler_params=pltpu.CompilerParams(vmem_limit_bytes=32 * 2**20),
        cost_estimate=pl.CostEstimate(
            flops=2 * RING * count * model * wide,
            bytes_accessed=2 * RING * (count * (model + wide) + model * wide),
            transcendentals=RING * count * wide,
        ),
    )(which, packed, *pieces)


def unpack_kernel(rows, where_ref, spread_ref, answers_ref, first_ref, out_ref):
    slots = GROUPS * CAP
    tile = GROUPS * rows
    for start in range(0, spread_ref.shape[0], tile):
        part = start // tile * slots
        held = [answers_ref[i, part : part + slots] for i in range(RING)]
        out = jnp.dot(
            spread_ref[start : start + tile],
            jnp.concatenate(held + held),
            preferred_element_type=jnp.float32,
        )
        out_ref[0, start : start + tile] = out.astype(out_ref.dtype)


def unpack_across_kernel(rows, where_ref, spread_ref, answers_ref, first_ref, out_ref):
    tile = spread_ref.shape[2]
    for block in range(RING):
        held = [answers_ref[i, block, 0] for i in range(RING)]
        out = jnp.dot(
            spread_ref[block, 0], jnp.concatenate(held + held), preferred_element_type=jnp.float32
        )
        out_ref[0, block * tile : (block + 1) * tile] = out.astype(out_ref.dtype)


def unpack(where, spread, answers, part, axis, rows, dtype, first):
    blocks = where.shape[0]
    count, wide = spread.shape[0] // RING, spread.shape[1]
    slots, columns = answers.shape[1] // RING, part[1] - part[0]
    column = part[0] // columns
    if axis == "y":
        kernel = unpack_kernel
        spread_spec = pl.BlockSpec((count, wide), lambda i, where: (where[i], 0))
        answers_spec = pl.BlockSpec((RING, slots, columns), lambda i, where: (0, where[i], column))
    else:
        kernel = unpack_across_kernel
        spread = spread.reshape(RING, RING, count // RING, wide)
        answers = answers.reshape(RING, RING, 2, slots // 2, answers.shape[2])
        spread_spec = pl.BlockSpec((RING, 1, count // RING, wide), lambda i, where: (0, where[i], 0, 0))
        answers_spec = pl.BlockSpec(
            (RING, RING, 1, slots // 2, columns), lambda i, where: (0, 0, where[i] // 2, 0, column)
        )
    return pl.pallas_call(
        functools.partial(kernel, rows),
        grid_spec=pltpu.PrefetchScalarGridSpec(
            num_scalar_prefetch=1,
            grid=(blocks,),
            in_specs=[spread_spec, answers_spec, pl.BlockSpec(memory_space=pl.ANY)],
            out_specs=pl.BlockSpec((1, count, columns), lambda i, where: (i, 0, 0)),
        ),
        out_shape=jax.ShapeDtypeStruct((blocks, count, columns), dtype),
        compiler_params=pltpu.CompilerParams(vmem_limit_bytes=18 * 2**20),
        cost_estimate=pl.CostEstimate(
            flops=2 * blocks * count * wide * columns,
            bytes_accessed=2 * blocks * count * (wide + 2 * columns),
            transcendentals=0,
        ),
    )(where, spread, answers, first)


def local(deltas, master, momentum, hidden, expert_ids, gate_weights):
    experts, block_rows, width = deltas.shape[1:]
    sub = master.shape[3]
    steps, rows, model = hidden.shape
    top = expert_ids.shape[2]
    z_lo, core = lax.axis_index("z_lo"), lax.axis_index("core")
    y, x, z_hi = lax.axis_index("y"), lax.axis_index("x"), lax.axis_index("z_hi")
    z = z_hi * 2 + z_lo
    taken = steps * rows
    owners = RING * RING
    span = owners * sub
    cut = width // 2

    pieces = deltas[0].reshape(experts, 2, 2, sub, width)
    kept = lax.dynamic_index_in_dim(pieces, core, axis=2, keepdims=False)
    given = lax.dynamic_index_in_dim(pieces, 1 - core, axis=2, keepdims=False)
    other = swap(given, "core")

    def pair(index):
        both = [lax.dynamic_index_in_dim(value, index, axis=1, keepdims=False) for value in (kept, other)]
        return both[0].astype(jnp.float32) + both[1].astype(jnp.float32)

    given = pair(1 - z_lo).astype(jnp.bfloat16)
    received = swap(given, "z_lo")
    hidden, expert_ids, gate_weights = [
        later(value, given) for value in (hidden, expert_ids, gate_weights)
    ]

    named = (expert_ids.reshape(taken, top)[:, :, None] == jnp.arange(experts)).astype(jnp.float32)
    row = jnp.arange(taken)
    earlier = (row[:, None] // rows == row // rows) & (row[:, None] > row)
    rank = jnp.dot(
        earlier.astype(jnp.bfloat16),
        jnp.sum(named, axis=1).astype(jnp.bfloat16),
        preferred_element_type=jnp.float32,
    )
    rank = jnp.sum(named * rank[:, None], axis=2).astype(jnp.int32).reshape(expert_ids.shape)
    group = (x % 2) * steps + jnp.arange(steps, dtype=jnp.int32)[:, None, None]
    slot = expert_ids % RING * (GROUPS * CAP) + group * CAP + rank
    gate_high = rounded(gate_weights)
    routing = jnp.concatenate(
        [(expert_ids // RING).astype(jnp.float32), slot.astype(jnp.float32), gate_high, gate_weights - gate_high],
        axis=-1,
    ).astype(jnp.bfloat16)
    routing = jnp.pad(routing.reshape(taken, 4 * top), ((0, 0), (0, LANES - 4 * top)))
    place = jnp.arange(model, dtype=jnp.int32)
    turn = place // span % CHIPS
    ring_z = z + jnp.where(turn < 3, turn - 1, jnp.where(turn % 2 == 1, -1, 1) * (turn // 2 + turn % 2))
    ring_z = (z + jnp.where(turn == 7, 4, ring_z - z)) % CHIPS
    ring_core = (core + place // (CHIPS * span)) % 2
    source = (place // sub % owners) * RING + ring_z // 2
    source = source * block_rows + (ring_z % 2) * 2 * sub + ring_core * sub + place % sub
    ordering = (jnp.arange(model, dtype=jnp.int32)[:, None] == source[None, :]).astype(jnp.bfloat16)
    flat = jnp.dot(
        hidden.reshape(taken, model), ordering, preferred_element_type=jnp.float32
    ).astype(jnp.bfloat16)
    flat = jnp.concatenate([flat, routing], axis=1)
    flat = with_layout_constraint(flat, Layout(major_to_minor=(0, 1)))

    plane = lax.all_gather(flat, ("y", "x"), axis=0, tiled=True)
    params = master.reshape(experts, sub, width)
    velocity_old = momentum.reshape(experts, sub, width)
    outer_grad = (pair(z_lo) + received.astype(jnp.float32)) / 4
    velocity = outer_momentum * velocity_old + outer_grad
    piece = (params - outer_rate * (outer_grad + outer_momentum * velocity)).astype(jnp.bfloat16)

    piece = piece.reshape(owners, RING, sub, width).transpose(0, 2, 1, 3).reshape(owners, sub, RING * width)
    piece = lax.all_to_all(piece, ("y", "x"), split_axis=0, concat_axis=0, tiled=True)
    piece = piece.reshape(span, RING * width)

    def hop(up, down):
        return lax.ppermute(up, Z, UP), lax.ppermute(down, Z, DOWN)

    hops = [(piece, piece)]
    for _ in range(3):
        hops.append(hop(*hops[-1]))
    here = (y * RING + x).reshape(1)
    packed, spread = pack(here, plane, model, top, rows)
    up, down = passed_on(hops[3], spread)
    low, high = hop(up[: span // 2], down[span // 2 :])
    (up1, down1), (up2, down2) = hops[1:3]
    first = [up1, piece, down1]
    rest = [up2, down2, up, down, low, high]
    pieces = first + rest + [swap(jnp.concatenate(first), "core")] + [swap(part, "core") for part in rest]
    answers, engine = answers_of(z_hi.reshape(1), packed, pieces)

    def last_ring(summed, axis, at):
        summed = summed.reshape(RING, taken, -1)
        own, before, after, far = [
            lax.dynamic_index_in_dim(summed, (at + offset) % RING, axis=0, keepdims=False)
            for offset in (0, 3, 1, 2)
        ]
        received = [
            lax.ppermute(far.astype(jnp.bfloat16), axis, [(i, (i + 2) % RING) for i in range(RING)]),
            lax.ppermute(after.astype(jnp.bfloat16), axis, PLUS),
            lax.ppermute(before.astype(jnp.bfloat16), axis, MINUS),
        ]
        for value in received:
            own = own + value.astype(jnp.float32)
        return own

    ways = [((0, cut), "y", y, "x", x), ((cut, width), "x", x, "y", y)]
    first = spread
    fars, nears, decoded = [], [], []
    for part, axis, at, _, _ in ways:
        block = ((at + 2) % RING).reshape(1)
        first = unpack(block, spread, answers, part, axis, rows, jnp.bfloat16, first)
        fars.append(first)
    for part, axis, at, _, _ in ways:
        near_blocks = (at + jnp.array([3, 1, 0], jnp.int32)) % RING
        first = unpack(near_blocks, spread, answers, part, axis, rows, jnp.float32, first)
        nears.append(first)
    for far, terms, (_, axis, _, second, at) in zip(fars, nears, ways):
        before, after = far_sums(terms[0], terms[1], far[0], axis)
        decoded.append(last_ring(near_sums(terms[2], before, after, axis), second, at))
    (engine,) = passed_on([engine], before)
    decoded = jnp.concatenate(decoded, axis=1).reshape(steps, rows, width).astype(jnp.bfloat16)

    engine = engine.reshape(2, CHIPS, owners, sub, width)
    engine = by_core(core, engine[:1], engine[1:], 0)
    engine = jnp.concatenate([engine[:, i : i + 1] for i in (5, 3, 0, 1, 2, 4, 6, 7)] * 2, axis=1)
    engine = lax.dynamic_slice_in_dim(engine, (CHIPS + 3 - z) % CHIPS, CHIPS, axis=1)
    engine = engine.transpose(2, 1, 0, 3, 4).reshape(model, width)
    return (engine[None], velocity.reshape(momentum.shape), decoded)


def solution(mesh):
    fine = Mesh(
        mesh.devices.reshape(2, 2, RING, RING, RING), ("z_lo", "core", "y", "x", "z_hi")
    )
    rep, ep = ("z_lo", "core"), ("y", "x", "z_hi")
    return jax.shard_map(
        local,
        mesh=fine,
        in_specs=(
            P(rep, None, ep, None),
            P(None, ep, rep, None, None),
            P(None, ep, rep, None, None),
            P(None, rep + ep, None),
            P(None, rep + ep, None),
            P(None, rep + ep, None),
        ),
        out_specs=(
            P(ep, None, None),
            P(None, ep, rep, None, None),
            P(None, rep + ep, None),
        ),
        check_vma=False,
    )
```
